256 devices in a mesh: row: 8 (over x_lo, y), col: 32 (over z, x_hi, core).
Axes of the slice: x: 4 (x_hi: 2, x_lo: 2; x = x_hi * 2 + x_lo), y: 4, z: 8, core: 2. Of those that a mesh axis runs over, the one named last changes fastest.
Arguments:
- markov: bfloat16 [8192, 8192], P('row', 'col'), may hold values from 0.049804688 to 1
- input_tiles: int32 [64, 64], P('row', 'col'), may hold values from 0 to 1, as said below
- keep_tiles: int32 [64, 64], P('row', 'col'), may hold values from 0 to 1, as said below
Outputs:
- clustered: bfloat16 [8192, 8192], P('row', 'col')
The draws below stay inside these ranges and needn't reach their ends.
Inputs may be any that keep to these rules, and one draw needn't show every extreme that they name: `input_tiles`: entries are 0 or 1; every diagonal tile is 1. Each device's block of 8 x 2 tiles holds at most 8 ones, and some block holds exactly 8. `keep_tiles`: entries are 0 or 1; every diagonal tile is 1.
All inputs are finite; a program needn't handle non-finite values.
Results may differ from the reference program's by a relative error of at most 0.001.
Values may be sent and summed in bfloat16 or wider, within the bound.
A program may use at most 128 MiB of HBM per device.

```python
import math
import jax
import jax.numpy as jnp

TILE = 128
CT_DEV = 2
NTILES = 64
RT_DEV = 8
MOST_BLK = 8
ORDER = 8192
N_ROW = 8
N_COL = 32


def diagonal_ones():
    rows = jnp.arange(NTILES, dtype=jnp.int32)
    return rows[:, None] == rows[None, :]


def draw_input_tiles(key, part):
    key = jax.random.fold_in(key, 11)
    first, second, third, fourth = jax.random.split(key, 4)
    heavy_rows = (jax.random.permutation(first, NTILES) < max(NTILES // 16, 1)).astype(jnp.int32)
    scores = jax.random.randint(second, (NTILES, NTILES), 0, 1000)
    scores = scores + 1000 * heavy_rows[:, None] + 4000 * diagonal_ones().astype(jnp.int32)
    flat_index = jnp.arange(NTILES * NTILES, dtype=jnp.int32).reshape(NTILES, NTILES)
    ranked = scores * (NTILES * NTILES) + flat_index
    blocks = ranked.reshape(N_ROW, RT_DEV, N_COL, CT_DEV).transpose(0, 2, 1, 3).reshape(N_ROW * N_COL, RT_DEV * CT_DEV)
    order_in = jnp.argsort(-blocks, axis=1)
    position = jnp.argsort(order_in, axis=1)
    counts = jax.random.randint(third, (N_ROW * N_COL,), MOST_BLK // 2, MOST_BLK + 1)
    chosen = jax.random.randint(fourth, (), 0, N_ROW * N_COL)
    counts = jnp.where(jnp.arange(N_ROW * N_COL, dtype=jnp.int32) == chosen, MOST_BLK, counts)
    kept = (position < counts[:, None]).astype(jnp.int32)
    return kept.reshape(N_ROW, N_COL, RT_DEV, CT_DEV).transpose(0, 2, 1, 3).reshape(NTILES, NTILES)


def draw_keep_tiles(key, part):
    key = jax.random.fold_in(key, 23)
    rolled = jax.random.randint(key, (NTILES, NTILES), 0, 100)
    return ((rolled < 50) | diagonal_ones()).astype(jnp.int32)


def block_levels(rng, shape, pieces, smallest, top_value):
    loudness = 1.0
    for dim, blocks in pieces:
        heights = jax.random.uniform(jax.random.fold_in(jax.random.fold_in(rng, 6), dim), (blocks,), jnp.float32, smallest / len(pieces), top_value / len(pieces))
        loudness = loudness * jnp.repeat(jnp.exp(heights), shape[dim] // blocks).reshape((-1,) + (1,) * (len(shape) - 1 - dim))
    return loudness


def setup_inputs(seed: int = 0) -> dict:
    key_list = jax.random.split(jax.random.key(seed), 4)
    return {
        "markov": jnp.clip(jnp.exp(math.log(1.0) - 2.9996462 * jax.random.uniform(key_list[0], (ORDER, ORDER), jnp.float32) ** block_levels(key_list[0], (ORDER, ORDER), ((0, 8), (1, 32)), -0.2, 0.2)), 0.049804688, 1.0).astype(jnp.bfloat16),
        "input_tiles": draw_input_tiles(jax.random.fold_in(key_list[3], 71), 0),
        "keep_tiles": draw_keep_tiles(jax.random.fold_in(key_list[3], 71), 0),
    }


def spread(pattern):
    return jnp.repeat(jnp.repeat(pattern, TILE, axis=0), TILE, axis=1)


def reference(markov, input_tiles, keep_tiles):
    masked = markov * spread(input_tiles).astype(jnp.bfloat16)
    square = jnp.dot(masked, masked, preferred_element_type=jnp.float32)
    inflated = square * square * spread(keep_tiles).astype(jnp.float32)
    colsum = jnp.sum(inflated, axis=0)
    return (jnp.float32(ORDER) * inflated / colsum[None, :]).astype(jnp.bfloat16)
```

```python
import jax
import jax.numpy as jnp
from jax import lax
from jax.experimental import pallas as pl
from jax.experimental.pallas import tpu as pltpu
from jax.sharding import PartitionSpec as P

MESH = pl.DeviceIdType.MESH
T = 128
RT, CT = 8, 2
SLOTS = 8
PT = 4
NZ, NY, NROW = 8, 4, 8
BLOCK = RT * T
COPIES = 96


def kernel(mk, it, kt, out, g0, g1, g2, g3, g4, g5, g6, g7, col, rhs, lhs, acc, cs, tabs, ctabs, ssem, rsem):
    groups = (g0, g1, g2, g3, g4, g5, g6, g7)
    me_row, me_col = lax.axis_index("row"), lax.axis_index("col")
    xlo, y = me_row // NY, me_row % NY
    z, xh, core = me_col // 4, (me_col // 2) % 2, me_col % 2

    def zdev(d):
        return (me_row, ((z + d + NZ) % NZ) * 4 + xh * 2 + core)

    def ydev(d):
        return (xlo * NY + (y + d + NY) % NY, me_col)

    xdev = (me_row, z * 4 + (1 - xh) * 2 + core)
    xldev = ((1 - xlo) * NY + y, me_col)
    cdev = (me_row, z * 4 + xh * 2 + (1 - core))
    peers = [((me_row + j) % NROW, me_col) for j in range(1, NROW)]

    barrier = pltpu.get_barrier_semaphore()
    for dev in [zdev(1), zdev(-1), xdev, cdev] + peers:
        pl.semaphore_signal(barrier, inc=1, device_id=dev, device_id_type=MESH)

    count = [0]
    started = []

    def send(src, dst, dev):
        k = count[0]
        count[0] += 1
        copy = pltpu.make_async_remote_copy(
            src_ref=src, dst_ref=dst, send_sem=ssem.at[k], recv_sem=rsem.at[k], device_id=dev, device_id_type=MESH
        )
        copy.start()
        started.append(copy)
        return copy

    def drain():
        for copy in started:
            copy.wait_send()
        started.clear()

    e0, e1 = core * 2 + xh, core * 2 + (1 - xh)
    front, back, whole = pl.ds(0, PT), pl.ds(PT, SLOTS - PT), pl.ds(0, SLOTS)

    seen = jnp.int32(0)
    place = [(jnp.int32(0), jnp.int32(0))] * SLOTS
    for p in range(RT * CT):
        there = it[p // CT, p % CT] > 0
        slot = jnp.where(there, seen, SLOTS)
        tabs[core * 16 + xh, p] = slot
        ctabs[me_row, p] = slot
        for s in range(min(p + 1, SLOTS)):
            i, k = place[s]
            place[s] = (jnp.where(slot == s, p // CT, i), jnp.where(slot == s, p % CT, k))
        seen = seen + there.astype(jnp.int32)
    for s in range(SLOTS):
        i, k = place[s]
        tile = jnp.where(k == 0, mk[i, :, :T], mk[i, :, T:])
        g0[e0, s] = tile
        col[me_row, s] = tile

    pl.semaphore_wait(barrier, 4 + len(peers))

    px = send(g0.at[e0, front], g0.at[e0, front], xdev)
    tx = send(tabs.at[pl.ds(core * 16 + xh, 1)], tabs.at[pl.ds(core * 16 + xh, 1)], xdev)
    up = {0: groups[0], 1: groups[1], 2: groups[2], 3: groups[3], 4: groups[4]}
    down = {0: groups[0], 1: groups[5], 2: groups[6], 3: groups[7], 4: groups[4]}
    half_f, half_b = PT // 2, (SLOTS - PT) // 2

    def ring(e, lo, n, d):
        if d < 4:
            a = b = pl.ds(lo, n)
        else:
            a, b = pl.ds(lo, n // 2), pl.ds(lo + n // 2, n - n // 2)
        return (
            send(up[d - 1].at[e, a], up[d].at[e, a], zdev(1)),
            send(down[d - 1].at[e, b], down[d].at[e, b], zdev(-1)),
        )

    def arrived(copies):
        for copy in copies:
            copy.wait_recv()

    A, B, C = {}, {}, {}
    Q = {}
    K = {}

    def cross(rel):
        Q[rel] = send(groups[rel].at[e0, back], groups[rel].at[e0, back], xdev)

    def hand(rel):
        src = groups[rel].at[pl.ds(core * 2, 2), whole]
        K[rel] = send(src, src, cdev)

    A[1] = ring(e0, PT, SLOTS - PT, 1)
    xl = send(col.at[me_row, whole], col.at[me_row, whole], xldev)
    y1 = [send(col.at[me_row, whole], col.at[me_row, whole], ydev(d)) for d in (1, -1)]
    B[1] = ring(e0, 0, PT, 1)
    cross(0)
    ct = [send(ctabs.at[pl.ds(me_row, 1)], ctabs.at[pl.ds(me_row, 1)], dev) for dev in peers]

    zero = jnp.zeros((T, T), jnp.bfloat16)
    for g in groups:
        for e in range(4):
            g[e, SLOTS] = zero
    for b in range(NROW):
        col[b, SLOTS] = zero

    def tab(rel):
        return tabs.at[pl.ds(core * 16 + rel * 2, 2)]

    tx.wait_recv()
    tu = send(tab(0), tab(1), zdev(1))
    td = send(tab(0), tab(5), zdev(-1))

    px.wait_recv()
    C[1] = ring(e1, 0, PT, 1)
    arrived(A[1])
    A[2] = ring(e0, PT, SLOTS - PT, 2)
    cross(1)
    cross(5)
    arrived((tu, td))
    tu = send(tab(1), tab(2), zdev(1))
    td = send(tab(5), tab(6), zdev(-1))

    xl.wait_recv()
    other = (1 - xlo) * NY + y
    y1x = [send(col.at[other, whole], col.at[other, whole], ydev(d)) for d in (1, -1)]
    arrived(B[1])
    B[2] = ring(e0, 0, PT, 2)
    arrived(y1)
    lo, hi = pl.ds(0, SLOTS // 2), pl.ds(SLOTS // 2, SLOTS // 2)

    def second(x):
        below, above = x * NY + (y + NY - 1) % NY, x * NY + (y + 1) % NY
        return [
            send(col.at[below, lo], col.at[below, lo], ydev(1)),
            send(col.at[above, hi], col.at[above, hi], ydev(-1)),
        ]

    y2 = second(xlo)
    Q[0].wait_recv()
    hand(0)
    arrived((tu, td))
    tu = send(tab(2), tab(3), zdev(1))
    td = send(tab(6), tab(7), zdev(-1))
    arrived(A[2])
    A[3] = ring(e0, PT, SLOTS - PT, 3)
    cross(2)
    cross(6)
    arrived(C[1])
    C[2] = ring(e1, 0, PT, 2)
    arrived((tu, td))
    tu = send(tab(3), tab(4), zdev(1))
    arrived(B[2])
    B[3] = ring(e0, 0, PT, 3)
    arrived(y1x)
    y2x = second(1 - xlo)
    tu.wait_recv()
    mine = tabs.at[pl.ds(core * 16, 16)]
    tc = send(mine, mine, cdev)
    arrived(ct)
    Q[1].wait_recv()
    hand(1)
    Q[5].wait_recv()
    hand(5)
    arrived(A[3])
    A[4] = ring(e0, PT, SLOTS - PT, 4)
    cross(3)
    cross(7)
    arrived(y2)
    arrived(y2x)

    def column(b, _):
        def step(i, _):
            for k in range(CT):
                rhs[pl.ds(pl.multiple_of(b * BLOCK + i * T, T), T), k * T : (k + 1) * T] = col[b, ctabs[b, i * CT + k]]
            return 0

        return lax.fori_loop(0, RT, step, 0)

    def multiply(rel, owner, first=False):
        K[rel].wait_recv()
        g = groups[rel]

        def unpack(i, _):
            for c in range(2):
                for h in range(2):
                    for k in range(CT):
                        slot = tabs[c * 16 + rel * 2 + h, i * CT + k]
                        at = h * 512 + c * 256 + k * T
                        lhs[pl.ds(pl.multiple_of(i * T, T), T), at : at + T] = g[c * 2 + h, slot]
            return 0

        lax.fori_loop(0, RT, unpack, 0)

        def dot(m, _):
            rows = pl.ds(pl.multiple_of(m * 256, 256), 256)
            part = jnp.dot(
                lhs[rows, :],
                rhs[pl.ds(pl.multiple_of(owner * BLOCK, BLOCK), BLOCK), :],
                preferred_element_type=jnp.float32,
            )
            acc[rows, :] = part if first else acc[rows, :] + part
            return 0

        lax.fori_loop(0, BLOCK // 256, dot, 0)

    lax.fori_loop(0, NROW, column, 0)
    arrived(C[2])
    C[3] = ring(e1, 0, PT, 3)
    tc.wait_recv()
    multiply(0, z, first=True)
    arrived(B[3])
    B[4] = ring(e0, 0, PT, 4)
    multiply(1, (z + NZ - 1) % NZ)
    Q[2].wait_recv()
    hand(2)
    Q[6].wait_recv()
    hand(6)
    arrived(A[4])
    cross(4)
    arrived(C[3])
    C[4] = ring(e1, 0, PT, 4)
    multiply(5, (z + 1) % NZ)
    multiply(2, (z + NZ - 2) % NZ)
    multiply(6, (z + 2) % NZ)
    Q[3].wait_recv()
    hand(3)
    Q[7].wait_recv()
    hand(7)
    arrived(B[4])
    arrived(C[4])
    multiply(3, (z + NZ - 3) % NZ)
    multiply(7, (z + 3) % NZ)
    Q[4].wait_recv()
    hand(4)
    drain()
    multiply(4, (z + 4) % NZ)

    lane = lax.broadcasted_iota(jnp.int32, (1, CT * T), 1)

    def square(i, total):
        rows = pl.ds(pl.multiple_of(i * T, T), T)
        keep = jnp.where(lane < T, kt[i, 0], kt[i, 1]).astype(jnp.float32)
        v = acc[rows, :]
        v = v * v * keep
        acc[rows, :] = v
        return total + jnp.sum(v.reshape(T // 8, 8, CT * T), axis=0)

    cs[me_row] = lax.fori_loop(0, RT, square, jnp.zeros((8, CT * T), jnp.float32))
    sums = [send(cs.at[me_row], cs.at[me_row], dev) for dev in peers]
    arrived(sums)
    total = jnp.sum(jnp.sum(cs[...], axis=0), axis=0, keepdims=True)
    scale = jnp.float32(NZ * BLOCK) / total

    def finish(i, _):
        rows = pl.ds(pl.multiple_of(i * T, T), T)
        out[rows, :] = (acc[rows, :] * scale).astype(jnp.bfloat16)
        return 0

    lax.fori_loop(0, RT, finish, 0)
    drain()


def body(markov, input_tiles, keep_tiles):
    vmem, smem = pl.BlockSpec(memory_space=pltpu.VMEM), pl.BlockSpec(memory_space=pltpu.SMEM)
    return pl.pallas_call(
        kernel,
        out_shape=jax.ShapeDtypeStruct(markov.shape, jnp.bfloat16),
        in_specs=[vmem, smem, smem],
        out_specs=vmem,
        scratch_shapes=[pltpu.VMEM((4, SLOTS + 1, T, T), jnp.bfloat16)] * 8
        + [
            pltpu.VMEM((NROW, SLOTS + 1, T, T), jnp.bfloat16),
            pltpu.VMEM((NZ * BLOCK, CT * T), jnp.bfloat16),
            pltpu.VMEM((BLOCK, BLOCK), jnp.bfloat16),
            pltpu.VMEM((BLOCK, CT * T), jnp.float32),
            pltpu.VMEM((NROW, 8, CT * T), jnp.float32),
            pltpu.SMEM((32, 128), jnp.int32),
            pltpu.SMEM((NROW, 128), jnp.int32),
            pltpu.SemaphoreType.DMA((COPIES,)),
            pltpu.SemaphoreType.DMA((COPIES,)),
        ],
        compiler_params=pltpu.CompilerParams(
            collective_id=0, has_side_effects=True, vmem_limit_bytes=40 * 2**20
        ),
        name="cluster_step",
    )(markov.reshape(RT, T, CT * T), input_tiles, keep_tiles)


def solution(mesh):
    specs = (P("row", "col"), P("row", "col"), P("row", "col"))
    return jax.shard_map(body, mesh=mesh, in_specs=specs, out_specs=P("row", "col"), check_vma=False)
```

```python
import jax
import jax.numpy as jnp
from jax import lax
from jax.experimental import pallas as pl
from jax.experimental.pallas import tpu as pltpu
from jax.sharding import PartitionSpec as P

MESH = pl.DeviceIdType.MESH
T = 128
RT, CT = 8, 2
SLOTS = 8
HALF = T // 2
PACKED = 2 * SLOTS
FRONT = 9
NZ, NY, NROW = 8, 4, 8
BLOCK = RT * T
WIDTH = CT * T
COPIES = 96


def kernel(
    mk_hbm, it_hbm, kt_hbm, out, own0, own1, own2, own3, own4, far0, far1, far2, far3, far4, c0, cx, cy, cyx, c2, c2x,
    rhs, lhs, acc, cs, mk, it, kt, tabs, ctabs, insem, ssem, rsem,
):
    blocks = ((own0, own1, own2, own3, own4), (far0, far1, far2, far3, far4))
    me_row, me_col = lax.axis_index("row"), lax.axis_index("col")
    xlo, y = me_row // NY, me_row % NY
    z, xh, core = me_col // 4, (me_col // 2) % 2, me_col % 2
    zdevs = [(me_row, ((z + d) % NZ) * 4 + xh * 2 + core) for d in range(1, NZ)]
    up, down = zdevs[0], zdevs[-1]
    yup, ydown = [(xlo * NY + (y + d) % NY, me_col) for d in (1, NY - 1)]
    xdev = (me_row, z * 4 + (1 - xh) * 2 + core)
    xldev = ((1 - xlo) * NY + y, me_col)
    cdev = (me_row, z * 4 + xh * 2 + (1 - core))
    peers = [((me_row + j) % NROW, me_col) for j in range(1, NROW)]

    inputs = [(it_hbm, it), (mk_hbm, mk), (kt_hbm, kt)]
    fetch = [pltpu.make_async_copy(src, dst, insem.at[n]) for n, (src, dst) in enumerate(inputs)]
    for copy in fetch:
        copy.start()
    barrier = pltpu.get_barrier_semaphore()
    for dev in zdevs + [xdev, cdev] + peers:
        pl.semaphore_signal(barrier, inc=1, device_id=dev, device_id_type=MESH)

    count = [0]
    started = []

    def send(src, dst, dev):
        k = count[0]
        count[0] += 1
        copy = pltpu.make_async_remote_copy(
            src_ref=src, dst_ref=dst, send_sem=ssem.at[k], recv_sem=rsem.at[k], device_id=dev, device_id_type=MESH
        )
        copy.start()
        started.append(copy)
        return copy

    def drain(keep=0):
        while len(started) > keep:
            started.pop(0).wait_send()

    def arrived(copies):
        for copy in copies:
            copy.wait_recv()

    fetch[0].wait()
    seen = jnp.int32(0)
    place = [(jnp.int32(0), jnp.int32(0))] * SLOTS
    for p in range(RT * CT):
        there = it[p % CT, p // CT] > 0
        slot = jnp.where(there, seen, SLOTS)
        tabs[core * 16, p] = 2 * slot
        ctabs[me_row, p] = 2 * slot
        for s in range(min(p + 1, SLOTS)):
            i, k = place[s]
            place[s] = (jnp.where(slot == s, p // CT, i), jnp.where(slot == s, p % CT, k))
        seen = seen + there.astype(jnp.int32)
    fetch[1].wait()
    for s in range(SLOTS):
        i, k = place[s]
        tile = jnp.where(k == 0, mk[i, :, :T], mk[i, :, T:]).reshape(2, HALF, T)
        own0[0, core, 2 * s : 2 * s + 2] = tile
        c0[0, 2 * s : 2 * s + 2] = tile
    pl.semaphore_wait(barrier, len(zdevs) + 2 + len(peers))

    front, back, whole = (0, FRONT), (FRONT, PACKED - FRONT), (0, PACKED)
    streams = {"A": (0, back), "B": (0, front), "C": (1, front)}
    ring, crossed, handed = {}, {}, {}

    def at(d, side, o, part):
        return blocks[o][d].at[side % blocks[o][d].shape[0], core, pl.ds(*part)]

    def hop(name, d):
        o, (lo, n) = streams[name]
        h = n // 2
        lower, upper = (lo, h), (lo + h, n - h)
        if d > 1:
            arrived(ring[name, d - 1][0])
        parts = [(lower, upper)] if d == 4 else [(lower, upper), (upper, lower)] if d == 3 else [((lo, n), (lo, n))]
        pairs = [
            [send(at(d - 1, 0, o, a), at(d, 0, o, a), up), send(at(d - 1, 1, o, b), at(d, 1, o, b), down)] for a, b in parts
        ]
        ring[name, d] = (pairs[0], sum(pairs[1:], []))

    def ringed(name, d):
        first, rest = ring[name, d]
        arrived(first + rest if d == 4 else rest)

    def cross(d):
        src, dst = [blocks[o][d].at[:, core, pl.ds(*back)] for o in (0, 1)]
        crossed[d] = send(src, dst, xdev)

    def hand(d, o):
        src = blocks[o][d].at[:, core, pl.ds(*whole)]
        handed[d, o] = send(src, src, cdev)

    def column(ref, n, b):
        def step(i, _):
            for k in range(CT):
                rows = pl.ds(pl.multiple_of(b * BLOCK + i * T, T), T)
                rhs[rows, k * T : (k + 1) * T] = ref[n, pl.ds(ctabs[b, i * CT + k], 2)].reshape(T, T)
            return 0

        lax.fori_loop(0, RT, step, 0)

    def multiply(d, side, o, first=False):
        owner = (z + (NZ - d if side == 0 else d)) % NZ

        def unpack(i, _):
            for c in (0, 1):
                for k in range(CT):
                    slot = tabs[c * 16 + (d + 4 if side else d) * 2 + o, i * CT + k]
                    tile = blocks[o][d][side, c, pl.ds(slot, 2)].reshape(T, T)
                    lhs[pl.ds(pl.multiple_of(i * T, T), T), c * WIDTH + k * T : c * WIDTH + (k + 1) * T] = tile
            return 0

        lax.fori_loop(0, RT, unpack, 0)
        half = (1 - xh) if o else xh
        rows = pl.ds(pl.multiple_of(owner * BLOCK + half * (2 * WIDTH), 2 * WIDTH), 2 * WIDTH)
        part = jnp.dot(lhs[...], rhs[rows, :], preferred_element_type=jnp.float32)
        acc[...] = part if first else acc[...] + part

    tx = send(tabs.at[pl.ds(core * 16, 1)], tabs.at[pl.ds(core * 16 + 1, 1)], xdev)
    hop("A", 1)
    px = send(at(0, 0, 0, front), at(0, 0, 1, front), xdev)
    ct = [send(ctabs.at[pl.ds(me_row, 1)], ctabs.at[pl.ds(me_row, 1)], dev) for dev in peers]
    lower, upper = pl.ds(0, SLOTS), pl.ds(SLOTS, SLOTS)
    y1 = [send(c0.at[0, part], cy.at[n, part], dev) for n, dev, part in [(0, yup, lower), (1, ydown, upper)]]
    hop("B", 1)
    y1 += [send(c0.at[0, part], cy.at[n, part], dev) for n, dev, part in [(0, yup, upper), (1, ydown, lower)]]
    xl = [send(c0.at[0, part], cx.at[0, part], xldev) for part in (lower, upper)]
    hand(0, 0)
    cross(0)

    zero = jnp.zeros((2, HALF, T), jnp.bfloat16)
    for ref in blocks[0] + blocks[1]:
        for n in range(ref.shape[0]):
            for c in (0, 1):
                ref[n, c, PACKED : PACKED + 2] = zero
    for ref in (c0, cx, cy, cyx, c2, c2x):
        for n in range(ref.shape[0]):
            ref[n, PACKED : PACKED + 2] = zero

    tx.wait_recv()
    pair = tabs.at[pl.ds(core * 16, 2)]
    tz = []
    for j, dev in enumerate(zdevs):
        rel = j + 1 if j < 4 else 12 - (j + 1)
        tz.append(send(pair, tabs.at[pl.ds(core * 16 + rel * 2, 2)], dev))
    hop("A", 2)
    cross(1)
    px.wait_recv()
    hop("C", 1)
    arrived(y1[:2])
    y2 = [send(cy.at[0, lower], c2.at[0, lower], yup), send(cy.at[1, upper], c2.at[0, upper], ydown)]
    hop("B", 2)
    xl[0].wait_recv()
    y1x = [send(cx.at[0, lower], cyx.at[n, lower], dev) for n, dev in enumerate((yup, ydown))]
    arrived(ct)
    column(c0, 0, me_row)
    xl[1].wait_recv()
    y1x += [send(cx.at[0, upper], cyx.at[n, upper], dev) for n, dev in enumerate((yup, ydown))]
    hand(1, 0)
    hop("A", 3)
    cross(2)
    below, above, across = (y + NY - 1) % NY, (y + 1) % NY, (y + 2) % NY
    column(cx, 0, (1 - xlo) * NY + y)
    arrived(y1[2:])
    column(cy, 0, xlo * NY + below)
    column(cy, 1, xlo * NY + above)
    hop("C", 2)
    arrived([y1x[0], y1x[3]])
    y2x = [send(cyx.at[0, lower], c2x.at[0, lower], yup), send(cyx.at[1, upper], c2x.at[0, upper], ydown)]
    arrived(tz)
    mine = tabs.at[pl.ds(core * 16, 16)]
    tc = send(mine, mine, cdev)
    crossed[0].wait_recv()
    hand(0, 1)
    arrived(y1x[1:3])
    column(cyx, 0, (1 - xlo) * NY + below)
    column(cyx, 1, (1 - xlo) * NY + above)
    hop("B", 3)
    hand(2, 0)
    arrived(y2)
    column(c2, 0, xlo * NY + across)
    hop("A", 4)
    ringed("A", 3)
    cross(3)
    crossed[1].wait_recv()
    hand(1, 1)
    drain(20)
    arrived(y2x)
    column(c2x, 0, (1 - xlo) * NY + across)
    tc.wait_recv()
    handed[0, 0].wait_recv()
    multiply(0, 0, 0, first=True)
    handed[1, 0].wait_recv()
    multiply(1, 0, 0)
    hop("C", 3)
    multiply(1, 1, 0)
    hop("B", 4)
    ringed("B", 3)
    hand(3, 0)
    crossed[2].wait_recv()
    hand(2, 1)
    handed[2, 0].wait_recv()
    multiply(2, 0, 0)
    multiply(2, 1, 0)
    ringed("A", 4)
    cross(4)
    handed[0, 1].wait_recv()
    multiply(0, 0, 1)
    hop("C", 4)
    handed[1, 1].wait_recv()
    multiply(1, 0, 1)
    multiply(1, 1, 1)
    handed[2, 1].wait_recv()
    ringed("C", 3)
    crossed[3].wait_recv()
    hand(3, 1)
    multiply(2, 0, 1)
    multiply(2, 1, 1)
    ringed("B", 4)
    hand(4, 0)
    handed[3, 0].wait_recv()
    multiply(3, 0, 0)
    multiply(3, 1, 0)
    crossed[4].wait_recv()
    ringed("C", 4)
    hand(4, 1)
    drain(2)
    handed[3, 1].wait_recv()
    multiply(3, 0, 1)
    multiply(3, 1, 1)
    handed[4, 0].wait_recv()
    multiply(4, 0, 0)
    handed[4, 1].wait_recv()
    multiply(4, 0, 1)

    lane = lax.broadcasted_iota(jnp.int32, (1, WIDTH), 1)
    fetch[2].wait()

    def square(i, total):
        rows = pl.ds(pl.multiple_of(i * T, T), T)
        keep = jnp.where(lane < T, kt[0, i], kt[1, i]).astype(jnp.float32)
        v = acc[rows, :]
        v = v * v * keep
        acc[rows, :] = v
        return total + jnp.sum(v.reshape(T // 8, 8, WIDTH), axis=0)

    cs[me_row] = lax.fori_loop(0, RT, square, jnp.zeros((8, WIDTH), jnp.float32))
    sums = [send(cs.at[me_row], cs.at[me_row], dev) for dev in peers]
    drain(len(sums))
    arrived(sums)
    total = jnp.sum(jnp.sum(cs[...], axis=0), axis=0, keepdims=True)
    scale = jnp.float32(NZ * BLOCK) / total

    def finish(i, _):
        rows = pl.ds(pl.multiple_of(i * T, T), T)
        out[rows, :] = (acc[rows, :] * scale).astype(jnp.bfloat16)
        return 0

    lax.fori_loop(0, RT, finish, 0)
    drain()


def body(markov, input_tiles, keep_tiles):
    hbm = pl.BlockSpec(memory_space=pltpu.HBM)

    def packed(*lead):
        return pltpu.VMEM((*lead, PACKED + 2, HALF, T), jnp.bfloat16)

    sides = [packed(1, 2), packed(2, 2), packed(2, 2), packed(2, 2), packed(1, 2)]

    return pl.pallas_call(
        kernel,
        out_shape=jax.ShapeDtypeStruct(markov.shape, jnp.bfloat16),
        in_specs=[hbm, hbm, hbm],
        out_specs=pl.BlockSpec(memory_space=pltpu.VMEM),
        scratch_shapes=sides + sides
        + [packed(1), packed(1), packed(2), packed(2), packed(1), packed(1)]
        + [
            pltpu.VMEM((NZ * BLOCK, WIDTH), jnp.bfloat16),
            pltpu.VMEM((BLOCK, 2 * WIDTH), jnp.bfloat16),
            pltpu.VMEM((BLOCK, WIDTH), jnp.float32),
            pltpu.VMEM((NROW, 8, WIDTH), jnp.float32),
            pltpu.VMEM((RT, T, WIDTH), jnp.bfloat16),
            pltpu.SMEM((CT, RT), jnp.int32),
            pltpu.SMEM((CT, RT), jnp.int32),
            pltpu.SMEM((32, 128), jnp.int32),
            pltpu.SMEM((NROW, 128), jnp.int32),
            pltpu.SemaphoreType.DMA((3,)),
            pltpu.SemaphoreType.DMA((COPIES,)),
            pltpu.SemaphoreType.DMA((COPIES,)),
        ],
        compiler_params=pltpu.CompilerParams(
            collective_id=0, has_side_effects=True, vmem_limit_bytes=40 * 2**20
        ),
        name="cluster_step",
    )(markov.reshape(RT, T, WIDTH), input_tiles.T, keep_tiles.T)


def solution(mesh):
    specs = (P("row", "col"), P("row", "col"), P("row", "col"))
    return jax.shard_map(body, mesh=mesh, in_specs=specs, out_specs=P("row", "col"), check_vma=False)
```

```python
import jax
import jax.numpy as jnp
from jax import lax
from jax.experimental import pallas as pl
from jax.experimental.pallas import tpu as pltpu
from jax.sharding import PartitionSpec as P

MESH = pl.DeviceIdType.MESH
T = 128
RT, CT = 8, 2
SLOTS = 8
HALF = T // 2
PACKED = 2 * SLOTS
FRONT = 9
NZ, NY, NROW = 8, 4, 8
BLOCK = RT * T
WIDTH = CT * T
COPIES = 112
EARLY = 6


def kernel(
    mk_hbm, it_hbm, kt_hbm, out, own0, own1, own2, own3, own4, far0, far1, far2, far3, mine4, theirs4, c0, cx, cy, cyx, c2, c2x,
    rhs, lhs, acc, cs, mk, it, kt, tabs, ctabs, insem, ssem, rsem,
):
    blocks = ((own0, own1, own2, own3, own4), (far0, far1, far2, far3, None))
    me_row, me_col = lax.axis_index("row"), lax.axis_index("col")
    xlo, y = me_row // NY, me_row % NY
    z, xh, core = me_col // 4, (me_col // 2) % 2, me_col % 2
    zdevs = [(me_row, ((z + d) % NZ) * 4 + xh * 2 + core) for d in range(1, NZ)]
    up, down = zdevs[0], zdevs[-1]
    at_y = [[(x * NY + (y + d) % NY, me_col) for d in range(NY)] for x in (xlo, 1 - xlo)]
    yup, ydown = at_y[0][1], at_y[0][3]
    xdev = (me_row, z * 4 + (1 - xh) * 2 + core)
    xldev = at_y[1][0]
    cdev = (me_row, z * 4 + xh * 2 + (1 - core))
    peers = at_y[0][1:] + at_y[1]

    inputs = [(it_hbm, it), (mk_hbm, mk), (kt_hbm, kt)]
    fetch = [pltpu.make_async_copy(src, dst, insem.at[n]) for n, (src, dst) in enumerate(inputs)]
    for copy in fetch:
        copy.start()
    barrier = pltpu.get_barrier_semaphore()
    near = [up, down, xdev, cdev, yup, ydown, xldev]
    for dev in near:
        pl.semaphore_signal(barrier, inc=1, device_id=dev, device_id_type=MESH)

    count = [0]
    started = []

    def send(src, dst, dev):
        k = count[0]
        count[0] += 1
        copy = pltpu.make_async_remote_copy(
            src_ref=src, dst_ref=dst, send_sem=ssem.at[k], recv_sem=rsem.at[k], device_id=dev, device_id_type=MESH
        )
        copy.start()
        started.append(copy)
        return copy

    def drain(keep=0):
        while len(started) > keep:
            started.pop(0).wait_send()

    def arrived(copies):
        for copy in copies:
            copy.wait_recv()

    fetch[0].wait()
    seen = jnp.int32(0)
    place = [(jnp.int32(0), jnp.int32(0))] * SLOTS
    for p in range(RT * CT):
        there = it[p % CT, p // CT] > 0
        slot = jnp.where(there, seen, SLOTS)
        tabs[core * 16, p] = 2 * slot
        ctabs[me_row, p] = 2 * slot
        for s in range(min(p + 1, SLOTS)):
            i, k = place[s]
            place[s] = (jnp.where(slot == s, p // CT, i), jnp.where(slot == s, p % CT, k))
        seen = seen + there.astype(jnp.int32)
    fetch[1].wait()
    for s in range(SLOTS):
        i, k = place[s]
        tile = jnp.where(k == 0, mk[i, :, :T], mk[i, :, T:]).reshape(2, HALF, T)
        own0[0, core, 2 * s : 2 * s + 2] = tile
        c0[0, 2 * s : 2 * s + 2] = tile
    pl.semaphore_wait(barrier, len(near))

    front, back, whole = (0, FRONT), (FRONT, PACKED - FRONT), (0, PACKED)
    streams = {"A": (0, back), "B": (0, front), "C": (1, front)}
    ring, crossed, handed = {}, {}, {}

    def at(d, side, o, part):
        if o and d == 4:
            return mine4.at[pl.ds(*part)]
        return blocks[o][d].at[side % blocks[o][d].shape[0], core, pl.ds(*part)]

    def halves_of(name):
        o, (lo, n) = streams[name]
        return (lo, n // 2), (lo + n // 2, n - n // 2)

    def rel(d, side):
        return max(2 * d - 1, 0) + (side if 0 < d < 4 else 0)

    def table_of(o, d, side, n=1, c=core):
        return tabs.at[pl.ds(c * 16 + o * 8 + rel(d, side), n)]

    def both(name, d, a, b):
        o = streams[name][0]
        return [send(at(d - 1, 0, o, a), at(d, 0, o, a), up), send(at(d - 1, 1, o, b), at(d, 1, o, b), down)]

    def hop(name, d):
        if d > 1:
            arrived(ring[name, d - 1])
        if name != "B":
            o = streams[name][0]
            arrived(ring.get((name, "table", d - 1), []))
            ways = [(0, up), (1, down)][: 2 if d < 4 else 1]
            ring[name, "table", d] = [send(table_of(o, d - 1, side), table_of(o, d, side), dev) for side, dev in ways]
        whole = streams[name][1]
        ring[name, d] = both(name, d, *(halves_of(name) if d > 2 else (whole, whole)))

    def rest(name):
        ring[name, "rest"] = both(name, 3, *reversed(halves_of(name)))

    def cross(d):
        if d == 4:
            src, dst = at(4, 0, 0, back), at(4, 0, 1, back)
        else:
            src, dst = [blocks[o][d].at[:, core, pl.ds(*back)] for o in (0, 1)]
        crossed[d] = send(src, dst, xdev)

    def hand(d, o):
        table = table_of(o, d, 0, 2 if 0 < d < 4 else 1)
        src = blocks[o][d].at[:, core, pl.ds(*whole)]
        handed[d, o] = [send(table, table, cdev), send(src, src, cdev)]

    def column(ref, n, b):
        def step(i, _):
            for k in range(CT):
                rows = pl.ds(pl.multiple_of(b * BLOCK + i * T, T), T)
                rhs[rows, k * T : (k + 1) * T] = ref[n, pl.ds(ctabs[b, i * CT + k], 2)].reshape(T, T)
            return 0

        lax.fori_loop(0, RT, step, 0)

    place_of = {}

    def unpack(d, side, o, turn=None):
        place_of[d, side, o] = n = len(place_of) if turn is None else EARLY + turn

        def step(i, _):
            for c in (0, 1):
                for k in range(CT):
                    slot = tabs[c * 16 + o * 8 + rel(d, side), i * CT + k]
                    tile = blocks[o][d][side, c, pl.ds(slot, 2)].reshape(T, T)
                    lhs[n, pl.ds(pl.multiple_of(i * T, T), T), c * WIDTH + k * T : c * WIDTH + (k + 1) * T] = tile
            return 0

        lax.fori_loop(0, RT, step, 0)

    def multiply(d, side, o, first=False):
        owner = (z + (NZ - d if side == 0 else d)) % NZ
        half = (1 - xh) if o else xh
        rows = pl.ds(pl.multiple_of(owner * BLOCK + half * (2 * WIDTH), 2 * WIDTH), 2 * WIDTH)
        part = jnp.dot(lhs[place_of[d, side, o]], rhs[rows, :], preferred_element_type=jnp.float32)
        acc[...] = part if first else acc[...] + part

    def late(d, side, o):
        unpack(d, side, o, side)
        multiply(d, side, o)

    def multiply_last(ref, c):
        def step(i, _):
            for k in range(CT):
                tile = ref[pl.ds(tabs[c * 16 + 8 + rel(4, 0), i * CT + k], 2)].reshape(T, T)
                lhs[EARLY, pl.ds(pl.multiple_of(i * T, T), T), k * T : (k + 1) * T] = tile
            return 0

        lax.fori_loop(0, RT, step, 0)
        base = ((z + 4) % NZ) * BLOCK + (1 - xh) * (2 * WIDTH) + c * WIDTH
        rows = pl.ds(pl.multiple_of(base, WIDTH), WIDTH)
        acc[...] += jnp.dot(lhs[EARLY, :, :WIDTH], rhs[rows, :], preferred_element_type=jnp.float32)

    def ctable(b, devs):
        return [send(ctabs.at[pl.ds(b, 1)], ctabs.at[pl.ds(b, 1)], dev) for dev in devs]

    hop("A", 1)
    tx = send(table_of(0, 0, 0), table_of(1, 0, 0), xdev)
    px = send(at(0, 0, 0, front), at(0, 0, 1, front), xdev)
    lower, upper = pl.ds(0, SLOTS), pl.ds(SLOTS, SLOTS)
    ct = ctable(me_row, [yup, ydown])
    y1 = [send(c0.at[0, part], cy.at[n, part], dev) for n, dev, part in [(0, yup, lower), (1, ydown, upper)]]
    hop("B", 1)
    y1 += [send(c0.at[0, part], cy.at[n, part], dev) for n, dev, part in [(0, yup, upper), (1, ydown, lower)]]
    ctx = ctable(me_row, [xldev])
    xl = [send(c0.at[0, part], cx.at[0, part], xldev) for part in (lower, upper)]
    hand(0, 0)
    cross(0)

    zero = jnp.zeros((2, HALF, T), jnp.bfloat16)
    for ref in blocks[0] + blocks[1][:4]:
        for n in range(ref.shape[0]):
            for c in (0, 1):
                ref[n, c, PACKED : PACKED + 2] = zero
    for ref in (mine4, theirs4):
        ref[PACKED : PACKED + 2] = zero
    for ref in (c0, cx, cy, cyx, c2, c2x):
        for n in range(ref.shape[0]):
            ref[n, PACKED : PACKED + 2] = zero

    below, above, across = (y + NY - 1) % NY, (y + 1) % NY, (y + 2) % NY
    other = (1 - xlo) * NY
    hop("A", 2)
    cross(1)
    arrived([tx, px])
    hop("C", 1)
    arrived(y1[:2] + ct)
    ct2 = ctable(xlo * NY + below, [yup])
    y2 = [send(cy.at[0, lower], c2.at[0, lower], yup), send(cy.at[1, upper], c2.at[0, upper], ydown)]
    hop("B", 2)
    hand(1, 0)
    arrived(ctx + xl[:1])
    ctyx = ctable(other + y, [yup, ydown])
    y1x = [send(cx.at[0, lower], cyx.at[n, lower], dev) for n, dev in enumerate((yup, ydown))]
    column(c0, 0, me_row)
    hop("A", 3)
    rest("A")
    cross(2)
    arrived(xl[1:])
    y1x += [send(cx.at[0, upper], cyx.at[n, upper], dev) for n, dev in enumerate((yup, ydown))]
    column(cx, 0, other + y)
    arrived(y1[2:])
    column(cy, 0, xlo * NY + below)
    column(cy, 1, xlo * NY + above)
    arrived(handed[0, 0])
    unpack(0, 0, 0)
    hop("C", 2)
    crossed[0].wait_recv()
    hand(0, 1)
    arrived(handed[1, 0])
    unpack(1, 0, 0)
    unpack(1, 1, 0)
    arrived([y1x[0], y1x[3]] + ctyx)
    ct2x = ctable(other + below, [yup])
    y2x = [send(cyx.at[0, lower], c2x.at[0, lower], yup), send(cyx.at[1, upper], c2x.at[0, upper], ydown)]
    hop("B", 3)
    hand(2, 0)
    arrived(y1x[1:3])
    column(cyx, 0, other + below)
    column(cyx, 1, other + above)
    hop("A", 4)
    arrived(ring["A", "rest"])
    cross(3)
    arrived(handed[0, 1])
    unpack(0, 0, 1)
    arrived(y2 + ct2)
    column(c2, 0, xlo * NY + across)
    crossed[1].wait_recv()
    hand(1, 1)
    arrived(handed[2, 0])
    unpack(2, 0, 0)
    unpack(2, 1, 0)
    drain(24)
    arrived(y2x + ct2x)
    column(c2x, 0, other + across)
    multiply(0, 0, 0, first=True)
    hop("C", 3)
    rest("B")
    rest("C")
    multiply(1, 0, 0)
    multiply(1, 1, 0)
    multiply(0, 0, 1)
    hop("B", 4)
    drain(20)
    crossed[2].wait_recv()
    hand(2, 1)
    multiply(2, 0, 0)
    multiply(2, 1, 0)
    arrived(ring["A", 4])
    cross(4)
    arrived(handed[1, 1])
    late(1, 0, 1)
    late(1, 1, 1)
    hop("C", 4)
    drain(16)
    arrived(ring["B", "rest"])
    hand(3, 0)
    arrived(handed[2, 1])
    late(2, 0, 1)
    late(2, 1, 1)
    arrived(ring["C", "rest"])
    crossed[3].wait_recv()
    hand(3, 1)
    arrived(handed[3, 0])
    late(3, 0, 0)
    late(3, 1, 0)
    arrived(ring["B", 4] + ring["A", "table", 4])
    hand(4, 0)
    drain(12)
    arrived(handed[3, 1])
    late(3, 0, 1)

    def hand_last(lo, n):
        return send(mine4.at[pl.ds(lo, n)], theirs4.at[pl.ds(lo, n)], cdev)

    crossed[4].wait_recv()
    last = [hand_last(*back)]
    late(3, 1, 1)
    for copy, part in zip(ring["C", 4], halves_of("C")):
        copy.wait_recv()
        last.append(hand_last(*part))
    arrived(ring["C", "table", 4])
    last.append(send(table_of(1, 4, 0), table_of(1, 4, 0), cdev))
    arrived(handed[4, 0])
    late(4, 0, 0)
    multiply_last(mine4, core)
    drain(4)
    arrived(last)
    multiply_last(theirs4, 1 - core)

    lane = lax.broadcasted_iota(jnp.int32, (1, WIDTH), 1)
    fetch[2].wait()

    def square(i, total):
        rows = pl.ds(pl.multiple_of(i * T, T), T)
        keep = jnp.where(lane < T, kt[0, i], kt[1, i]).astype(jnp.float32)
        v = acc[rows, :]
        v = v * v * keep
        acc[rows, :] = v
        return total + jnp.sum(v.reshape(T // 8, 8, WIDTH), axis=0)

    part = lax.fori_loop(0, RT, square, jnp.zeros((8, WIDTH), jnp.float32))
    cs[me_row] = jnp.sum(part, axis=0, keepdims=True)
    sums = [send(cs.at[me_row], cs.at[me_row], dev) for dev in peers]
    drain(len(sums))
    arrived(sums)
    total = jnp.sum(cs[...], axis=0)
    scale = jnp.float32(NZ * BLOCK) / total

    def finish(i, _):
        rows = pl.ds(pl.multiple_of(i * T, T), T)
        out[rows, :] = (acc[rows, :] * scale).astype(jnp.bfloat16)
        return 0

    lax.fori_loop(0, RT, finish, 0)
    drain()


def body(markov, input_tiles, keep_tiles):
    hbm = pl.BlockSpec(memory_space=pltpu.HBM)

    def packed(*lead):
        return pltpu.VMEM((*lead, PACKED + 2, HALF, T), jnp.bfloat16)

    sides = [packed(1, 2), packed(2, 2), packed(2, 2), packed(2, 2), packed(1, 2)]

    return pl.pallas_call(
        kernel,
        out_shape=jax.ShapeDtypeStruct(markov.shape, jnp.bfloat16),
        in_specs=[hbm, hbm, hbm],
        out_specs=pl.BlockSpec(memory_space=pltpu.VMEM),
        scratch_shapes=sides + sides[:4]
        + [packed(), packed()]
        + [packed(1), packed(1), packed(2), packed(2), packed(1), packed(1)]
        + [
            pltpu.VMEM((NZ * BLOCK, WIDTH), jnp.bfloat16),
            pltpu.VMEM((EARLY + 2, BLOCK, 2 * WIDTH), jnp.bfloat16),
            pltpu.VMEM((BLOCK, WIDTH), jnp.float32),
            pltpu.VMEM((NROW, 1, WIDTH), jnp.float32),
            pltpu.VMEM((RT, T, WIDTH), jnp.bfloat16),
            pltpu.SMEM((CT, RT), jnp.int32),
            pltpu.SMEM((CT, RT), jnp.int32),
            pltpu.SMEM((32, 128), jnp.int32),
            pltpu.SMEM((NROW, 128), jnp.int32),
            pltpu.SemaphoreType.DMA((3,)),
            pltpu.SemaphoreType.DMA((COPIES,)),
            pltpu.SemaphoreType.DMA((COPIES,)),
        ],
        compiler_params=pltpu.CompilerParams(
            collective_id=0, has_side_effects=True, vmem_limit_bytes=53 * 2**20
        ),
        name="cluster_step",
    )(markov.reshape(RT, T, WIDTH), input_tiles.T, keep_tiles.T)


def solution(mesh):
    specs = (P("row", "col"), P("row", "col"), P("row", "col"))
    return jax.shard_map(body, mesh=mesh, in_specs=specs, out_specs=P("row", "col"), check_vma=False)
```

```python
import jax
import jax.numpy as jnp
from jax import lax
from jax.experimental import pallas as pl
from jax.experimental.pallas import tpu as pltpu
from jax.sharding import PartitionSpec as P

MESH = pl.DeviceIdType.MESH
T = 128
RT, CT = 8, 2
SLOTS = 8
HALF = T // 2
PACKED = 2 * SLOTS
FRONT = 9
NZ, NY, NROW = 8, 4, 8
BLOCK = RT * T
WIDTH = CT * T
COPIES = 112
EARLY = 6


def kernel(
    mk_hbm, it_hbm, kt_hbm, out, own0, own1, own2, own3, own4, far0, far1, far2, far3, mine4, theirs4, c0, cx, cy, cyx, c2, c2x,
    rhs, lhs, acc, cs, mk, it, kt, tabs, ctabs, insem, ssem, rsem,
):
    blocks = ((own0, own1, own2, own3, own4), (far0, far1, far2, far3, None))
    me_row, me_col = lax.axis_index("row"), lax.axis_index("col")
    xlo, y = me_row // NY, me_row % NY
    z, xh, core = me_col // 4, (me_col // 2) % 2, me_col % 2
    zdevs = [(me_row, ((z + d) % NZ) * 4 + xh * 2 + core) for d in range(1, NZ)]
    up, down = zdevs[0], zdevs[-1]
    at_y = [[(x * NY + (y + d) % NY, me_col) for d in range(NY)] for x in (xlo, 1 - xlo)]
    yup, ydown = at_y[0][1], at_y[0][3]
    xdev = (me_row, z * 4 + (1 - xh) * 2 + core)
    xldev = at_y[1][0]
    cdev = (me_row, z * 4 + xh * 2 + (1 - core))
    peers = [at_y[x][d] for x, d in ((1, 2), (1, 1), (1, 3), (0, 2), (1, 0), (0, 1), (0, 3))]

    barrier = pltpu.get_barrier_semaphore()
    near = [up, down, xdev, cdev, yup, ydown, xldev]
    for dev in near:
        pl.semaphore_signal(barrier, inc=1, device_id=dev, device_id_type=MESH)
    inputs = [(it_hbm, it), (kt_hbm, kt)]
    inputs += [(mk_hbm.at[:, :, pl.ds(k * T, T)], mk.at[pl.ds(k * RT, RT)]) for k in range(CT)]
    fetch = [pltpu.make_async_copy(src, dst, insem.at[n]) for n, (src, dst) in enumerate(inputs)]
    for n in (0, 2, 3, 1):
        fetch[n].start()

    count = [0]
    started = []

    def send(src, dst, dev):
        k = count[0]
        count[0] += 1
        copy = pltpu.make_async_remote_copy(
            src_ref=src, dst_ref=dst, send_sem=ssem.at[k], recv_sem=rsem.at[k], device_id=dev, device_id_type=MESH
        )
        copy.start()
        started.append(copy)
        return copy

    def drain(keep=0):
        while len(started) > keep:
            started.pop(0).wait_send()

    def arrived(copies):
        for copy in copies:
            copy.wait_recv()

    fetch[0].wait()
    seen = jnp.int32(0)
    place = [jnp.int32(0)] * SLOTS
    for p in range(RT * CT):
        i, k = p // CT, p % CT
        there = it[k, i] > 0
        slot = jnp.where(there, seen, SLOTS)
        tabs[core * 16, p] = 2 * slot
        ctabs[me_row, p] = 2 * slot
        for s in range(min(p + 1, SLOTS)):
            place[s] = jnp.where(slot == s, k * RT + i, place[s])
        seen = seen + there.astype(jnp.int32)
    fetch[2].wait()
    fetch[3].wait()
    for s in range(SLOTS):
        tile = mk[place[s]].reshape(2, HALF, T)
        own0[0, core, 2 * s : 2 * s + 2] = tile
        c0[0, 2 * s : 2 * s + 2] = tile
    pl.semaphore_wait(barrier, len(near))

    front, back, whole = (0, FRONT), (FRONT, PACKED - FRONT), (0, PACKED)
    streams = {"A": (0, back), "B": (0, front), "C": (1, front)}
    ring, crossed, handed = {}, {}, {}

    def at(d, side, o, part):
        if o and d == 4:
            return mine4.at[pl.ds(*part)]
        return blocks[o][d].at[side % blocks[o][d].shape[0], core, pl.ds(*part)]

    def halves_of(name):
        o, (lo, n) = streams[name]
        return (lo, n // 2), (lo + n // 2, n - n // 2)

    def rel(d, side):
        return max(2 * d - 1, 0) + (side if 0 < d < 4 else 0)

    def table_of(o, d, side, n=1, c=core):
        return tabs.at[pl.ds(c * 16 + o * 8 + rel(d, side), n)]

    def both(name, d, a, b):
        o = streams[name][0]
        return [send(at(d - 1, 0, o, a), at(d, 0, o, a), up), send(at(d - 1, 1, o, b), at(d, 1, o, b), down)]

    def hop(name, d):
        if d > 1:
            arrived(ring[name, d - 1])
        if name != "B":
            o = streams[name][0]
            arrived(ring.get((name, "table", d - 1), []))
            ways = [(0, up), (1, down)][: 2 if d < 4 else 1]
            ring[name, "table", d] = [send(table_of(o, d - 1, side), table_of(o, d, side), dev) for side, dev in ways]
        whole = streams[name][1]
        ring[name, d] = both(name, d, *(halves_of(name) if d > 2 else (whole, whole)))

    def rest(name):
        ring[name, "rest"] = both(name, 3, *reversed(halves_of(name)))

    def cross(d):
        if d == 4:
            src, dst = at(4, 0, 0, back), at(4, 0, 1, back)
        else:
            src, dst = [blocks[o][d].at[:, core, pl.ds(*back)] for o in (0, 1)]
        crossed[d] = send(src, dst, xdev)

    def hand(d, o):
        table = table_of(o, d, 0, 2 if 0 < d < 4 else 1)
        src = blocks[o][d].at[:, core, pl.ds(*whole)]
        handed[d, o] = [send(table, table, cdev), send(src, src, cdev)]

    def column(ref, n, b):
        def step(i, _):
            for k in range(CT):
                rows = pl.ds(pl.multiple_of(b * BLOCK + i * T, T), T)
                rhs[rows, k * T : (k + 1) * T] = ref[n, pl.ds(ctabs[b, i * CT + k], 2)].reshape(T, T)
            return 0

        lax.fori_loop(0, RT, step, 0)

    place_of = {}

    def unpack(d, side, o, turn=None, unroll=False):
        place_of[d, side, o] = n = len(place_of) if turn is None else EARLY + turn

        def step(i, _):
            for c in (0, 1):
                for k in range(CT):
                    slot = tabs[c * 16 + o * 8 + rel(d, side), i * CT + k]
                    tile = blocks[o][d][side, c, pl.ds(slot, 2)].reshape(T, T)
                    lhs[n, pl.ds(pl.multiple_of(i * T, T), T), c * WIDTH + k * T : c * WIDTH + (k + 1) * T] = tile
            return 0

        lax.fori_loop(0, RT, step, 0, unroll=unroll)

    def multiply(d, side, o, first=False):
        owner = (z + (NZ - d if side == 0 else d)) % NZ
        half = (1 - xh) if o else xh
        rows = pl.ds(pl.multiple_of(owner * BLOCK + half * (2 * WIDTH), 2 * WIDTH), 2 * WIDTH)
        part = jnp.dot(lhs[place_of[d, side, o]], rhs[rows, :], preferred_element_type=jnp.float32)
        acc[...] = part if first else acc[...] + part

    def late(d, side, o):
        unpack(d, side, o, side)
        multiply(d, side, o)

    def multiply_last(ref, c):
        def step(i, _):
            for k in range(CT):
                tile = ref[pl.ds(tabs[c * 16 + 8 + rel(4, 0), i * CT + k], 2)].reshape(T, T)
                lhs[EARLY, pl.ds(pl.multiple_of(i * T, T), T), k * T : (k + 1) * T] = tile
            return 0

        lax.fori_loop(0, RT, step, 0)
        base = ((z + 4) % NZ) * BLOCK + (1 - xh) * (2 * WIDTH) + c * WIDTH
        rows = pl.ds(pl.multiple_of(base, WIDTH), WIDTH)
        acc[...] += jnp.dot(lhs[EARLY, :, :WIDTH], rhs[rows, :], preferred_element_type=jnp.float32)

    def ctable(b, devs):
        return [send(ctabs.at[pl.ds(b, 1)], ctabs.at[pl.ds(b, 1)], dev) for dev in devs]

    hop("A", 1)
    tx = send(table_of(0, 0, 0), table_of(1, 0, 0), xdev)
    px = send(at(0, 0, 0, front), at(0, 0, 1, front), xdev)
    lower, upper = pl.ds(0, SLOTS), pl.ds(SLOTS, SLOTS)
    ct = ctable(me_row, [yup, ydown])
    y1 = [send(c0.at[0, part], cy.at[n, part], dev) for n, dev, part in [(0, yup, lower), (1, ydown, upper)]]
    hop("B", 1)
    y1 += [send(c0.at[0, part], cy.at[n, part], dev) for n, dev, part in [(0, yup, upper), (1, ydown, lower)]]
    ctx = ctable(me_row, [xldev])
    xl = [send(c0.at[0, part], cx.at[0, part], xldev) for part in (lower, upper)]
    hand(0, 0)
    cross(0)

    zero = jnp.zeros((2, HALF, T), jnp.bfloat16)
    for ref in blocks[0] + blocks[1][:4]:
        for n in range(ref.shape[0]):
            for c in (0, 1):
                ref[n, c, PACKED : PACKED + 2] = zero
    for ref in (mine4, theirs4):
        ref[PACKED : PACKED + 2] = zero
    for ref in (c0, cx, cy, cyx, c2, c2x):
        for n in range(ref.shape[0]):
            ref[n, PACKED : PACKED + 2] = zero

    below, above, across = (y + NY - 1) % NY, (y + 1) % NY, (y + 2) % NY
    other = (1 - xlo) * NY
    hop("A", 2)
    cross(1)
    arrived([tx, px])
    hop("C", 1)
    arrived(y1[:2] + ct)
    ct2 = ctable(xlo * NY + below, [yup])
    y2 = [send(cy.at[0, lower], c2.at[0, lower], yup), send(cy.at[1, upper], c2.at[0, upper], ydown)]
    hop("B", 2)
    hand(1, 0)
    arrived(ctx + xl[:1])
    ctyx = ctable(other + y, [yup, ydown])
    y1x = [send(cx.at[0, lower], cyx.at[n, lower], dev) for n, dev in enumerate((yup, ydown))]
    column(c0, 0, me_row)
    hop("A", 3)
    rest("A")
    cross(2)
    arrived(xl[1:])
    y1x += [send(cx.at[0, upper], cyx.at[n, upper], dev) for n, dev in enumerate((yup, ydown))]
    column(cx, 0, other + y)
    arrived(y1[2:])
    column(cy, 0, xlo * NY + below)
    column(cy, 1, xlo * NY + above)
    arrived(handed[0, 0])
    unpack(0, 0, 0)
    hop("C", 2)
    crossed[0].wait_recv()
    hand(0, 1)
    arrived(handed[1, 0])
    unpack(1, 0, 0)
    unpack(1, 1, 0)
    arrived([y1x[0], y1x[3]] + ctyx)
    ct2x = ctable(other + below, [yup])
    y2x = [send(cyx.at[0, lower], c2x.at[0, lower], yup), send(cyx.at[1, upper], c2x.at[0, upper], ydown)]
    hop("B", 3)
    hand(2, 0)
    arrived(y1x[1:3])
    column(cyx, 0, other + below)
    column(cyx, 1, other + above)
    hop("A", 4)
    arrived(ring["A", "rest"])
    cross(3)
    arrived(handed[0, 1])
    unpack(0, 0, 1)
    arrived(y2 + ct2)
    column(c2, 0, xlo * NY + across)
    crossed[1].wait_recv()
    hand(1, 1)
    arrived(handed[2, 0])
    unpack(2, 0, 0)
    unpack(2, 1, 0)
    drain(24)
    arrived(y2x + ct2x)
    column(c2x, 0, other + across)
    multiply(0, 0, 0, first=True)
    multiply(1, 0, 0)
    hop("C", 3)
    rest("B")
    rest("C")
    multiply(1, 1, 0)
    multiply(0, 0, 1)
    hop("B", 4)
    multiply(2, 0, 0)
    drain(20)
    crossed[2].wait_recv()
    hand(2, 1)
    multiply(2, 1, 0)
    arrived(handed[1, 1])
    late(1, 0, 1)
    arrived(ring["A", 4])
    cross(4)
    late(1, 1, 1)
    hop("C", 4)
    arrived(handed[2, 1])
    late(2, 0, 1)
    arrived(ring["B", "rest"])
    hand(3, 0)
    late(2, 1, 1)
    drain(16)
    arrived(ring["C", "rest"])
    crossed[3].wait_recv()
    hand(3, 1)
    arrived(handed[3, 0])
    unpack(3, 0, 0, 0)
    unpack(3, 1, 0, 1, unroll=True)
    multiply(3, 0, 0)
    multiply(3, 1, 0)
    arrived(ring["B", 4] + ring["A", "table", 4])
    hand(4, 0)
    drain(12)
    arrived(handed[3, 1])
    late(3, 0, 1)
    unpack(3, 1, 1, 1)

    def hand_last(lo, n):
        return send(mine4.at[pl.ds(lo, n)], theirs4.at[pl.ds(lo, n)], cdev)

    crossed[4].wait_recv()
    last = [hand_last(*back)]
    arrived(ring["C", "table", 4])
    last.append(send(table_of(1, 4, 0), table_of(1, 4, 0), cdev))
    for copy, part in zip(ring["C", 4], halves_of("C")):
        copy.wait_recv()
        last.append(hand_last(*part))
    arrived(handed[4, 0])
    unpack(4, 0, 0, 0, unroll=True)
    multiply(3, 1, 1)
    multiply(4, 0, 0)
    multiply_last(mine4, core)
    drain(4)
    arrived(last)
    multiply_last(theirs4, 1 - core)

    lane = lax.broadcasted_iota(jnp.int32, (1, WIDTH), 1)
    fetch[1].wait()

    def square(i, total):
        rows = pl.ds(pl.multiple_of(i * T, T), T)
        keep = jnp.where(lane < T, kt[0, i], kt[1, i]).astype(jnp.float32)
        v = acc[rows, :]
        v = v * v * keep
        acc[rows, :] = v
        return total + jnp.sum(v.reshape(T // 8, 8, WIDTH), axis=0)

    part = lax.fori_loop(0, RT, square, jnp.zeros((8, WIDTH), jnp.float32))
    cs[me_row] = jnp.sum(part, axis=0, keepdims=True)
    sums = [send(cs.at[me_row], cs.at[me_row], dev) for dev in peers]
    drain(len(sums))
    arrived(sums)
    total = jnp.sum(cs[...], axis=0)
    scale = jnp.float32(NZ * BLOCK) / total

    def finish(i, _):
        rows = pl.ds(pl.multiple_of(i * T, T), T)
        out[rows, :] = (acc[rows, :] * scale).astype(jnp.bfloat16)
        return 0

    lax.fori_loop(0, RT, finish, 0)
    drain()


def body(markov, input_tiles, keep_tiles):
    hbm = pl.BlockSpec(memory_space=pltpu.HBM)

    def packed(*lead):
        return pltpu.VMEM((*lead, PACKED + 2, HALF, T), jnp.bfloat16)

    sides = [packed(1, 2), packed(2, 2), packed(2, 2), packed(2, 2), packed(1, 2)]

    return pl.pallas_call(
        kernel,
        out_shape=jax.ShapeDtypeStruct(markov.shape, jnp.bfloat16),
        in_specs=[hbm, hbm, hbm],
        out_specs=pl.BlockSpec(memory_space=pltpu.VMEM),
        scratch_shapes=sides + sides[:4]
        + [packed(), packed()]
        + [packed(1), packed(1), packed(2), packed(2), packed(1), packed(1)]
        + [
            pltpu.VMEM((NZ * BLOCK, WIDTH), jnp.bfloat16),
            pltpu.VMEM((EARLY + 2, BLOCK, 2 * WIDTH), jnp.bfloat16),
            pltpu.VMEM((BLOCK, WIDTH), jnp.float32),
            pltpu.VMEM((NROW, 1, WIDTH), jnp.float32),
            pltpu.VMEM((CT * RT, T, T), jnp.bfloat16),
            pltpu.SMEM((CT, RT), jnp.int32),
            pltpu.SMEM((CT, RT), jnp.int32),
            pltpu.SMEM((32, 128), jnp.int32),
            pltpu.SMEM((NROW, 128), jnp.int32),
            pltpu.SemaphoreType.DMA((4,)),
            pltpu.SemaphoreType.DMA((COPIES,)),
            pltpu.SemaphoreType.DMA((COPIES,)),
        ],
        compiler_params=pltpu.CompilerParams(
            collective_id=0, has_side_effects=True, vmem_limit_bytes=53 * 2**20
        ),
        name="cluster_step",
    )(markov.reshape(RT, T, WIDTH), input_tiles.T, keep_tiles.T)


def solution(mesh):
    specs = (P("row", "col"), P("row", "col"), P("row", "col"))
    return jax.shard_map(body, mesh=mesh, in_specs=specs, out_specs=P("row", "col"), check_vma=False)
```

```python
import jax
import jax.numpy as jnp
from jax import lax
from jax.experimental import pallas as pl
from jax.experimental.pallas import tpu as pltpu
from jax.sharding import PartitionSpec as P

MESH = pl.DeviceIdType.MESH
T = 128
RT, CT = 8, 2
SLOTS = 8
HALF = T // 2
PACKED = 2 * SLOTS
FRONT = 9
NZ, NY, NROW = 8, 4, 8
BLOCK = RT * T
WIDTH = CT * T
COPIES = 112
EARLY = 6


def kernel(
    mk_hbm, it_hbm, kt_hbm, out, own0, own1, own2, own3, own4, far0, far1, far2, far3, mine4, theirs4, c0, cx, cy, cyx, c2, c2x,
    rhs, lhs, acc, cs, mk, it, kt, tabs, ctabs, insem, ssem, rsem,
):
    blocks = ((own0, own1, own2, own3, own4), (far0, far1, far2, far3, None))
    me_row, me_col = lax.axis_index("row"), lax.axis_index("col")
    xlo, y = me_row // NY, me_row % NY
    z, xh, core = me_col // 4, (me_col // 2) % 2, me_col % 2
    zdevs = [(me_row, ((z + d) % NZ) * 4 + xh * 2 + core) for d in range(1, NZ)]
    up, down = zdevs[0], zdevs[-1]
    at_y = [[(x * NY + (y + d) % NY, me_col) for d in range(NY)] for x in (xlo, 1 - xlo)]
    yup, ydown = at_y[0][1], at_y[0][3]
    xdev = (me_row, z * 4 + (1 - xh) * 2 + core)
    xldev = at_y[1][0]
    cdev = (me_row, z * 4 + xh * 2 + (1 - core))
    peers = [at_y[x][d] for x, d in ((1, 2), (1, 1), (1, 3), (0, 2), (1, 0), (0, 1), (0, 3))]

    barrier = pltpu.get_barrier_semaphore()
    near = [up, down, xdev, cdev, yup, ydown, xldev]
    for dev in near:
        pl.semaphore_signal(barrier, inc=1, device_id=dev, device_id_type=MESH)
    inputs = [(it_hbm, it), (kt_hbm, kt)]
    inputs += [(mk_hbm.at[:, :, pl.ds(k * T, T)], mk.at[pl.ds(k * RT, RT)]) for k in range(CT)]
    fetch = [pltpu.make_async_copy(src, dst, insem.at[n]) for n, (src, dst) in enumerate(inputs)]
    for n in (0, 2, 3, 1):
        fetch[n].start()

    count = [0]
    started = []

    def send(src, dst, dev):
        k = count[0]
        count[0] += 1
        copy = pltpu.make_async_remote_copy(
            src_ref=src, dst_ref=dst, send_sem=ssem.at[k], recv_sem=rsem.at[k], device_id=dev, device_id_type=MESH
        )
        copy.start()
        started.append(copy)
        return copy

    def drain(keep=0):
        while len(started) > keep:
            started.pop(0).wait_send()

    def arrived(copies):
        for copy in copies:
            copy.wait_recv()

    fetch[0].wait()
    seen = jnp.int32(0)
    place = [jnp.int32(0)] * SLOTS
    for p in range(RT * CT):
        i, k = p // CT, p % CT
        there = it[k, i] > 0
        slot = jnp.where(there, seen, SLOTS)
        tabs[core * 16, p] = 2 * slot
        ctabs[me_row, p] = 2 * slot
        for s in range(min(p + 1, SLOTS)):
            place[s] = jnp.where(slot == s, k * RT + i, place[s])
        seen = seen + there.astype(jnp.int32)
    fetch[2].wait()
    fetch[3].wait()
    for s in range(SLOTS):
        tile = mk[place[s]].reshape(2, HALF, T)
        own0[0, core, 2 * s : 2 * s + 2] = tile
        c0[0, 2 * s : 2 * s + 2] = tile
    pl.semaphore_wait(barrier, len(near))

    front, back, whole = (0, FRONT), (FRONT, PACKED - FRONT), (0, PACKED)
    streams = {"A": (0, back), "B": (0, front), "C": (1, front)}
    ring, crossed, handed = {}, {}, {}

    def at(d, side, o, part):
        if o and d == 4:
            return mine4.at[pl.ds(*part)]
        return blocks[o][d].at[side % blocks[o][d].shape[0], core, pl.ds(*part)]

    def halves_of(name):
        o, (lo, n) = streams[name]
        return (lo, n // 2), (lo + n // 2, n - n // 2)

    def rel(d, side):
        return max(2 * d - 1, 0) + (side if 0 < d < 4 else 0)

    def table_of(o, d, side, n=1, c=core):
        return tabs.at[pl.ds(c * 16 + o * 8 + rel(d, side), n)]

    def both(name, d, a, b):
        o = streams[name][0]
        return [send(at(d - 1, 0, o, a), at(d, 0, o, a), up), send(at(d - 1, 1, o, b), at(d, 1, o, b), down)]

    def hop(name, d):
        if d > 1:
            arrived(ring[name, d - 1])
        if name != "B":
            o = streams[name][0]
            arrived(ring.get((name, "table", d - 1), []))
            ways = [(0, up), (1, down)][: 2 if d < 4 else 1]
            ring[name, "table", d] = [send(table_of(o, d - 1, side), table_of(o, d, side), dev) for side, dev in ways]
        whole = streams[name][1]
        ring[name, d] = both(name, d, *(halves_of(name) if d > 2 else (whole, whole)))

    def rest(name):
        ring[name, "rest"] = both(name, 3, *reversed(halves_of(name)))

    def cross(d):
        if d == 4:
            src, dst = at(4, 0, 0, back), at(4, 0, 1, back)
        else:
            src, dst = [blocks[o][d].at[:, core, pl.ds(*back)] for o in (0, 1)]
        crossed[d] = send(src, dst, xdev)

    def hand(d, o):
        table = table_of(o, d, 0, 2 if 0 < d < 4 else 1)
        src = blocks[o][d].at[:, core, pl.ds(*whole)]
        handed[d, o] = [send(table, table, cdev), send(src, src, cdev)]

    def column(ref, n, b):
        def step(i, _):
            for k in range(CT):
                rows = pl.ds(pl.multiple_of(b * BLOCK + i * T, T), T)
                rhs[rows, k * T : (k + 1) * T] = ref[n, pl.ds(ctabs[b, i * CT + k], 2)].reshape(T, T)
            return 0

        lax.fori_loop(0, RT, step, 0)

    place_of = {}

    def unpack(d, side, o, turn=None, unroll=False):
        place_of[d, side, o] = n = len(place_of) if turn is None else EARLY + turn

        def step(i, _):
            for c in (0, 1):
                for k in range(CT):
                    slot = tabs[c * 16 + o * 8 + rel(d, side), i * CT + k]
                    tile = blocks[o][d][side, c, pl.ds(slot, 2)].reshape(T, T)
                    lhs[n, pl.ds(pl.multiple_of(i * T, T), T), c * WIDTH + k * T : c * WIDTH + (k + 1) * T] = tile
            return 0

        lax.fori_loop(0, RT, step, 0, unroll=unroll)

    def multiply(d, side, o, first=False):
        owner = (z + (NZ - d if side == 0 else d)) % NZ
        half = (1 - xh) if o else xh
        rows = pl.ds(pl.multiple_of(owner * BLOCK + half * (2 * WIDTH), 2 * WIDTH), 2 * WIDTH)
        part = jnp.dot(lhs[place_of[d, side, o]], rhs[rows, :], preferred_element_type=jnp.float32)
        acc[...] = part if first else acc[...] + part

    def late(d, side, o):
        unpack(d, side, o, side)
        multiply(d, side, o)

    def unpack_last(ref, c, n, unroll=False):
        def step(i, _):
            for k in range(CT):
                tile = ref[pl.ds(tabs[c * 16 + 8 + rel(4, 0), i * CT + k], 2)].reshape(T, T)
                lhs[n, pl.ds(pl.multiple_of(i * T, T), T), k * T : (k + 1) * T] = tile
            return 0

        lax.fori_loop(0, RT, step, 0, unroll=unroll)

    def multiply_last(c, n):
        base = ((z + 4) % NZ) * BLOCK + (1 - xh) * (2 * WIDTH) + c * WIDTH
        rows = pl.ds(pl.multiple_of(base, WIDTH), WIDTH)
        acc[...] += jnp.dot(lhs[n, :, :WIDTH], rhs[rows, :], preferred_element_type=jnp.float32)

    def ctable(b, devs):
        return [send(ctabs.at[pl.ds(b, 1)], ctabs.at[pl.ds(b, 1)], dev) for dev in devs]

    hop("A", 1)
    tx = send(table_of(0, 0, 0), table_of(1, 0, 0), xdev)
    px = send(at(0, 0, 0, front), at(0, 0, 1, front), xdev)
    lower, upper = pl.ds(0, SLOTS), pl.ds(SLOTS, SLOTS)
    ct = ctable(me_row, [yup, ydown])
    y1 = [send(c0.at[0, part], cy.at[n, part], dev) for n, dev, part in [(0, yup, lower), (1, ydown, upper)]]
    hop("B", 1)
    y1 += [send(c0.at[0, part], cy.at[n, part], dev) for n, dev, part in [(0, yup, upper), (1, ydown, lower)]]
    ctx = ctable(me_row, [xldev])
    xl = [send(c0.at[0, part], cx.at[0, part], xldev) for part in (lower, upper)]
    hand(0, 0)
    cross(0)

    zero = jnp.zeros((2, HALF, T), jnp.bfloat16)
    for ref in blocks[0] + blocks[1][:4]:
        for n in range(ref.shape[0]):
            for c in (0, 1):
                ref[n, c, PACKED : PACKED + 2] = zero
    for ref in (mine4, theirs4):
        ref[PACKED : PACKED + 2] = zero
    for ref in (c0, cx, cy, cyx, c2, c2x):
        for n in range(ref.shape[0]):
            ref[n, PACKED : PACKED + 2] = zero

    below, above, across = (y + NY - 1) % NY, (y + 1) % NY, (y + 2) % NY
    other = (1 - xlo) * NY
    hop("A", 2)
    cross(1)
    arrived([tx, px])
    hop("C", 1)
    arrived(y1[:2] + ct)
    ct2 = ctable(xlo * NY + below, [yup])
    y2 = [send(cy.at[0, lower], c2.at[0, lower], yup), send(cy.at[1, upper], c2.at[0, upper], ydown)]
    hop("B", 2)
    hand(1, 0)
    arrived(ctx + xl[:1])
    ctyx = ctable(other + y, [yup, ydown])
    y1x = [send(cx.at[0, lower], cyx.at[n, lower], dev) for n, dev in enumerate((yup, ydown))]
    column(c0, 0, me_row)
    hop("A", 3)
    rest("A")
    cross(2)
    arrived(xl[1:])
    y1x += [send(cx.at[0, upper], cyx.at[n, upper], dev) for n, dev in enumerate((yup, ydown))]
    column(cx, 0, other + y)
    arrived(y1[2:])
    column(cy, 0, xlo * NY + below)
    column(cy, 1, xlo * NY + above)
    arrived(handed[0, 0])
    unpack(0, 0, 0)
    hop("C", 2)
    crossed[0].wait_recv()
    hand(0, 1)
    arrived(handed[1, 0])
    unpack(1, 0, 0)
    unpack(1, 1, 0)
    arrived([y1x[0], y1x[3]] + ctyx)
    ct2x = ctable(other + below, [yup])
    y2x = [send(cyx.at[0, lower], c2x.at[0, lower], yup), send(cyx.at[1, upper], c2x.at[0, upper], ydown)]
    hop("B", 3)
    hand(2, 0)
    arrived(y1x[1:3])
    column(cyx, 0, other + below)
    column(cyx, 1, other + above)
    hop("A", 4)
    arrived(ring["A", "rest"])
    cross(3)
    arrived(handed[0, 1])
    unpack(0, 0, 1)
    arrived(y2 + ct2)
    column(c2, 0, xlo * NY + across)
    crossed[1].wait_recv()
    hand(1, 1)
    arrived(handed[2, 0])
    unpack(2, 0, 0)
    unpack(2, 1, 0)
    drain(24)
    arrived(y2x + ct2x)
    column(c2x, 0, other + across)
    multiply(0, 0, 0, first=True)
    multiply(1, 0, 0)
    hop("C", 3)
    rest("B")
    rest("C")
    multiply(1, 1, 0)
    multiply(0, 0, 1)
    hop("B", 4)
    multiply(2, 0, 0)
    drain(20)
    crossed[2].wait_recv()
    hand(2, 1)
    multiply(2, 1, 0)
    arrived(handed[1, 1])
    late(1, 0, 1)
    arrived(ring["A", 4])
    cross(4)
    late(1, 1, 1)
    hop("C", 4)
    arrived(handed[2, 1])
    late(2, 0, 1)
    arrived(ring["B", "rest"])
    hand(3, 0)
    late(2, 1, 1)
    drain(16)
    arrived(ring["C", "rest"])
    crossed[3].wait_recv()
    hand(3, 1)
    arrived(handed[3, 0])
    unpack(3, 0, 0, 0)
    unpack(3, 1, 0, 1, unroll=True)
    multiply(3, 0, 0)
    multiply(3, 1, 0)
    arrived(ring["B", 4] + ring["A", "table", 4])
    hand(4, 0)
    drain(12)
    arrived(handed[3, 1])
    late(3, 0, 1)
    unpack(3, 1, 1, 1)

    def hand_last(lo, n):
        return send(mine4.at[pl.ds(lo, n)], theirs4.at[pl.ds(lo, n)], cdev)

    crossed[4].wait_recv()
    last = [hand_last(*back)]
    arrived(ring["C", "table", 4])
    last.append(send(table_of(1, 4, 0), table_of(1, 4, 0), cdev))
    for copy, part in zip(ring["C", 4], halves_of("C")):
        copy.wait_recv()
        last.append(hand_last(*part))
    arrived(handed[4, 0])
    unpack(4, 0, 0, 0, unroll=True)
    multiply(3, 1, 1)
    unpack_last(mine4, core, 0, unroll=True)
    multiply(4, 0, 0)
    multiply_last(core, 0)
    drain(4)
    arrived(last)
    unpack_last(theirs4, 1 - core, 1, unroll=True)
    multiply_last(1 - core, 1)

    lane = lax.broadcasted_iota(jnp.int32, (1, WIDTH), 1)
    fetch[1].wait()

    def square(i, total):
        rows = pl.ds(pl.multiple_of(i * T, T), T)
        keep = jnp.where(lane < T, kt[0, i], kt[1, i]).astype(jnp.float32)
        v = acc[rows, :]
        v = v * v * keep
        acc[rows, :] = v
        return total + jnp.sum(v.reshape(T // 8, 8, WIDTH), axis=0)

    part = lax.fori_loop(0, RT, square, jnp.zeros((8, WIDTH), jnp.float32), unroll=True)
    cs[me_row] = jnp.sum(part, axis=0, keepdims=True)
    sums = [send(cs.at[me_row], cs.at[me_row], dev) for dev in peers]
    drain(len(sums))
    arrived(sums)
    total = jnp.sum(cs[...], axis=0)
    scale = jnp.float32(NZ * BLOCK) / total

    def finish(i, _):
        rows = pl.ds(pl.multiple_of(i * T, T), T)
        out[rows, :] = (acc[rows, :] * scale).astype(jnp.bfloat16)
        return 0

    lax.fori_loop(0, RT, finish, 0, unroll=True)
    drain()


def body(markov, input_tiles, keep_tiles):
    hbm = pl.BlockSpec(memory_space=pltpu.HBM)

    def packed(*lead):
        return pltpu.VMEM((*lead, PACKED + 2, HALF, T), jnp.bfloat16)

    sides = [packed(1, 2), packed(2, 2), packed(2, 2), packed(2, 2), packed(1, 2)]

    return pl.pallas_call(
        kernel,
        out_shape=jax.ShapeDtypeStruct(markov.shape, jnp.bfloat16),
        in_specs=[hbm, hbm, hbm],
        out_specs=pl.BlockSpec(memory_space=pltpu.VMEM),
        scratch_shapes=sides + sides[:4]
        + [packed(), packed()]
        + [packed(1), packed(1), packed(2), packed(2), packed(1), packed(1)]
        + [
            pltpu.VMEM((NZ * BLOCK, WIDTH), jnp.bfloat16),
            pltpu.VMEM((EARLY + 2, BLOCK, 2 * WIDTH), jnp.bfloat16),
            pltpu.VMEM((BLOCK, WIDTH), jnp.float32),
            pltpu.VMEM((NROW, 1, WIDTH), jnp.float32),
            pltpu.VMEM((CT * RT, T, T), jnp.bfloat16),
            pltpu.SMEM((CT, RT), jnp.int32),
            pltpu.SMEM((CT, RT), jnp.int32),
            pltpu.SMEM((32, 128), jnp.int32),
            pltpu.SMEM((NROW, 128), jnp.int32),
            pltpu.SemaphoreType.DMA((4,)),
            pltpu.SemaphoreType.DMA((COPIES,)),
            pltpu.SemaphoreType.DMA((COPIES,)),
        ],
        compiler_params=pltpu.CompilerParams(
            collective_id=0, has_side_effects=True, vmem_limit_bytes=53 * 2**20
        ),
        name="cluster_step",
    )(markov.reshape(RT, T, WIDTH), input_tiles.T, keep_tiles.T)


def solution(mesh):
    specs = (P("row", "col"), P("row", "col"), P("row", "col"))
    return jax.shard_map(body, mesh=mesh, in_specs=specs, out_specs=P("row", "col"), check_vma=False)
```

```python
import jax
import jax.numpy as jnp
from jax import lax
from jax.experimental import pallas as pl
from jax.experimental.pallas import tpu as pltpu
from jax.sharding import PartitionSpec as P

MESH = pl.DeviceIdType.MESH
T = 128
RT, CT = 8, 2
SLOTS = 8
HALF = T // 2
PACKED = 2 * SLOTS
FRONT = 9
NZ, NY, NROW = 8, 4, 8
BLOCK = RT * T
WIDTH = CT * T
COPIES = 112
EARLY = 6


def kernel(
    mk_hbm, it_hbm, kt_hbm, out, own0, own1, own2, own3, own4, far0, far1, far2, far3, mine4, theirs4, c0, cx, cy, cyx, c2, c2x,
    rhs, lhs, acc, cs, mk, it, kt, tabs, ctabs, insem, ssem, rsem,
):
    blocks = ((own0, own1, own2, own3, own4), (far0, far1, far2, far3, None))
    me_row, me_col = lax.axis_index("row"), lax.axis_index("col")
    xlo, y = me_row // NY, me_row % NY
    z, xh, core = me_col // 4, (me_col // 2) % 2, me_col % 2
    zdevs = [(me_row, ((z + d) % NZ) * 4 + xh * 2 + core) for d in range(1, NZ)]
    up, down = zdevs[0], zdevs[-1]
    at_y = [[(x * NY + (y + d) % NY, me_col) for d in range(NY)] for x in (xlo, 1 - xlo)]
    yup, ydown = at_y[0][1], at_y[0][3]
    xdev = (me_row, z * 4 + (1 - xh) * 2 + core)
    xldev = at_y[1][0]
    cdev = (me_row, z * 4 + xh * 2 + (1 - core))
    peers = [at_y[x][d] for x, d in ((1, 2), (1, 1), (1, 3), (0, 2), (1, 0), (0, 1), (0, 3))]

    barrier = pltpu.get_barrier_semaphore()
    near = [up, down, xdev, cdev, yup, ydown, xldev]
    for dev in near:
        pl.semaphore_signal(barrier, inc=1, device_id=dev, device_id_type=MESH)
    inputs = [(it_hbm, it), (kt_hbm, kt)]
    inputs += [(mk_hbm.at[:, :, pl.ds(k * T, T)], mk.at[pl.ds(k * RT, RT)]) for k in range(CT)]
    fetch = [pltpu.make_async_copy(src, dst, insem.at[n]) for n, (src, dst) in enumerate(inputs)]
    for n in (0, 2, 3, 1):
        fetch[n].start()

    count = [0]
    started = []

    def send(src, dst, dev):
        k = count[0]
        count[0] += 1
        copy = pltpu.make_async_remote_copy(
            src_ref=src, dst_ref=dst, send_sem=ssem.at[k], recv_sem=rsem.at[k], device_id=dev, device_id_type=MESH
        )
        copy.start()
        started.append(copy)
        return copy

    def drain(keep=0):
        while len(started) > keep:
            started.pop(0).wait_send()

    def arrived(copies):
        for copy in copies:
            copy.wait_recv()

    fetch[0].wait()
    seen = jnp.int32(0)
    place = [jnp.int32(0)] * SLOTS
    for p in range(RT * CT):
        i, k = p // CT, p % CT
        there = it[k, i] > 0
        slot = jnp.where(there, seen, SLOTS)
        tabs[core * 16, p] = 2 * slot
        ctabs[me_row, p] = 2 * slot
        for s in range(min(p + 1, SLOTS)):
            place[s] = jnp.where(slot == s, k * RT + i, place[s])
        seen = seen + there.astype(jnp.int32)
    fetch[2].wait()
    fetch[3].wait()
    for s in range(SLOTS):
        tile = mk[place[s]].reshape(2, HALF, T)
        own0[0, core, 2 * s : 2 * s + 2] = tile
        c0[0, 2 * s : 2 * s + 2] = tile
    pl.semaphore_wait(barrier, len(near))

    front, back, whole = (0, FRONT), (FRONT, PACKED - FRONT), (0, PACKED)
    streams = {"A": (0, back), "B": (0, front), "C": (1, front)}
    ring, crossed, handed = {}, {}, {}

    def at(d, side, o, part):
        if o and d == 4:
            return mine4.at[pl.ds(*part)]
        return blocks[o][d].at[side % blocks[o][d].shape[0], core, pl.ds(*part)]

    def halves_of(name):
        o, (lo, n) = streams[name]
        return (lo, n // 2), (lo + n // 2, n - n // 2)

    def rel(d, side):
        return max(2 * d - 1, 0) + (side if 0 < d < 4 else 0)

    def table_of(o, d, side, n=1, c=core):
        return tabs.at[pl.ds(c * 16 + o * 8 + rel(d, side), n)]

    def both(name, d, a, b):
        o = streams[name][0]
        return [send(at(d - 1, 0, o, a), at(d, 0, o, a), up), send(at(d - 1, 1, o, b), at(d, 1, o, b), down)]

    def hop(name, d):
        if d > 1:
            arrived(ring[name, d - 1])
        if name != "B":
            o = streams[name][0]
            arrived(ring.get((name, "table", d - 1), []))
            ways = [(0, up), (1, down)][: 2 if d < 4 else 1]
            ring[name, "table", d] = [send(table_of(o, d - 1, side), table_of(o, d, side), dev) for side, dev in ways]
        whole = streams[name][1]
        ring[name, d] = both(name, d, *(halves_of(name) if d > 2 else (whole, whole)))

    def rest(name):
        ring[name, "rest"] = both(name, 3, *reversed(halves_of(name)))

    def cross(d):
        if d == 4:
            src, dst = at(4, 0, 0, back), at(4, 0, 1, back)
        else:
            src, dst = [blocks[o][d].at[:, core, pl.ds(*back)] for o in (0, 1)]
        crossed[d] = send(src, dst, xdev)

    def hand(d, o):
        table = table_of(o, 0, 0, 5) if (d, o) == (2, 0) else table_of(o, d, 0, 2 if 0 < d < 4 else 1)
        src = blocks[o][d].at[:, core, pl.ds(*whole)]
        handed[d, o] = [] if o == 0 and d < 2 else [send(table, table, cdev)]
        handed[d, o].append(send(src, src, cdev))

    def column(ref, n, b):
        def step(i, _):
            for k in range(CT):
                rows = pl.ds(pl.multiple_of(b * BLOCK + i * T, T), T)
                rhs[rows, k * T : (k + 1) * T] = ref[n, pl.ds(ctabs[b, i * CT + k], 2)].reshape(T, T)
            return 0

        lax.fori_loop(0, RT, step, 0)

    place_of = {}

    def unpack(d, side, o, turn=None, unroll=False):
        place_of[d, side, o] = n = len(place_of) if turn is None else EARLY + turn

        def step(i, _):
            for c in (0, 1):
                for k in range(CT):
                    slot = tabs[c * 16 + o * 8 + rel(d, side), i * CT + k]
                    tile = blocks[o][d][side, c, pl.ds(slot, 2)].reshape(T, T)
                    lhs[n, pl.ds(pl.multiple_of(i * T, T), T), c * WIDTH + k * T : c * WIDTH + (k + 1) * T] = tile
            return 0

        lax.fori_loop(0, RT, step, 0, unroll=unroll)

    def multiply(d, side, o, first=False):
        owner = (z + (NZ - d if side == 0 else d)) % NZ
        half = (1 - xh) if o else xh
        rows = pl.ds(pl.multiple_of(owner * BLOCK + half * (2 * WIDTH), 2 * WIDTH), 2 * WIDTH)
        part = jnp.dot(lhs[place_of[d, side, o]], rhs[rows, :], preferred_element_type=jnp.float32)
        acc[...] = part if first else acc[...] + part

    def late(d, side, o):
        unpack(d, side, o, side)
        multiply(d, side, o)

    def unpack_last(ref, c, n, unroll=False):
        def step(i, _):
            for k in range(CT):
                tile = ref[pl.ds(tabs[c * 16 + 8 + rel(4, 0), i * CT + k], 2)].reshape(T, T)
                lhs[n, pl.ds(pl.multiple_of(i * T, T), T), k * T : (k + 1) * T] = tile
            return 0

        lax.fori_loop(0, RT, step, 0, unroll=unroll)

    def multiply_last(c, n):
        base = ((z + 4) % NZ) * BLOCK + (1 - xh) * (2 * WIDTH) + c * WIDTH
        rows = pl.ds(pl.multiple_of(base, WIDTH), WIDTH)
        acc[...] += jnp.dot(lhs[n, :, :WIDTH], rhs[rows, :], preferred_element_type=jnp.float32)

    def ctable(b, devs):
        return [send(ctabs.at[pl.ds(b, 1)], ctabs.at[pl.ds(b, 1)], dev) for dev in devs]

    hop("A", 1)
    tx = send(table_of(0, 0, 0), table_of(1, 0, 0), xdev)
    px = send(at(0, 0, 0, front), at(0, 0, 1, front), xdev)
    lower, upper = pl.ds(0, SLOTS), pl.ds(SLOTS, SLOTS)
    ct = ctable(me_row, [yup, ydown])
    y1 = [send(c0.at[0, pl.ds(*whole)], cy.at[n, pl.ds(*whole)], dev) for n, dev in enumerate((yup, ydown))]
    hop("B", 1)
    ctx = ctable(me_row, [xldev])
    xl = [send(c0.at[0, part], cx.at[0, part], xldev) for part in (lower, upper)]
    hand(0, 0)
    cross(0)

    zero = jnp.zeros((2, HALF, T), jnp.bfloat16)
    for ref in blocks[0] + blocks[1][:4]:
        for n in range(ref.shape[0]):
            for c in (0, 1):
                ref[n, c, PACKED : PACKED + 2] = zero
    for ref in (mine4, theirs4):
        ref[PACKED : PACKED + 2] = zero
    for ref in (c0, cx, cy, cyx, c2, c2x):
        for n in range(ref.shape[0]):
            ref[n, PACKED : PACKED + 2] = zero

    below, above, across = (y + NY - 1) % NY, (y + 1) % NY, (y + 2) % NY
    other = (1 - xlo) * NY
    hop("A", 2)
    cross(1)
    arrived([tx, px])
    hop("C", 1)
    arrived(y1 + ct)
    ct2 = ctable(xlo * NY + below, [yup])
    y2 = [send(cy.at[0, lower], c2.at[0, lower], yup), send(cy.at[1, upper], c2.at[0, upper], ydown)]
    hop("B", 2)
    hand(1, 0)
    arrived(ctx + xl[:1])
    ctyx = ctable(other + y, [yup, ydown])
    y1x = [send(cx.at[0, lower], cyx.at[n, lower], dev) for n, dev in enumerate((yup, ydown))]
    column(c0, 0, me_row)
    hop("A", 3)
    rest("A")
    cross(2)
    arrived(xl[1:])
    y1x += [send(cx.at[0, upper], cyx.at[n, upper], dev) for n, dev in enumerate((yup, ydown))]
    column(cx, 0, other + y)
    column(cy, 0, xlo * NY + below)
    column(cy, 1, xlo * NY + above)
    hop("C", 2)
    crossed[0].wait_recv()
    hand(0, 1)
    arrived([y1x[0], y1x[3]] + ctyx)
    ct2x = ctable(other + below, [yup])
    y2x = [send(cyx.at[0, lower], c2x.at[0, lower], yup), send(cyx.at[1, upper], c2x.at[0, upper], ydown)]
    hop("B", 3)
    hand(2, 0)
    arrived(y1x[1:3])
    column(cyx, 0, other + below)
    column(cyx, 1, other + above)
    hop("A", 4)
    arrived(ring["A", "rest"])
    cross(3)
    arrived(handed[0, 1])
    unpack(0, 0, 1)
    arrived(y2 + ct2)
    column(c2, 0, xlo * NY + across)
    crossed[1].wait_recv()
    hand(1, 1)
    arrived(handed[0, 0] + handed[1, 0] + handed[2, 0])
    unpack(0, 0, 0)
    unpack(1, 0, 0)
    unpack(1, 1, 0)
    unpack(2, 0, 0)
    unpack(2, 1, 0)
    drain(24)
    arrived(y2x + ct2x)
    column(c2x, 0, other + across)
    multiply(0, 0, 0, first=True)
    multiply(1, 0, 0)
    hop("C", 3)
    rest("B")
    rest("C")
    multiply(1, 1, 0)
    multiply(0, 0, 1)
    hop("B", 4)
    multiply(2, 0, 0)
    drain(20)
    crossed[2].wait_recv()
    hand(2, 1)
    multiply(2, 1, 0)
    arrived(handed[1, 1])
    late(1, 0, 1)
    arrived(ring["A", 4])
    cross(4)
    late(1, 1, 1)
    hop("C", 4)
    arrived(handed[2, 1])
    late(2, 0, 1)
    arrived(ring["B", "rest"])
    hand(3, 0)
    late(2, 1, 1)
    drain(16)
    arrived(ring["C", "rest"])
    crossed[3].wait_recv()
    hand(3, 1)
    arrived(handed[3, 0])
    unpack(3, 0, 0, 0)
    unpack(3, 1, 0, 1, unroll=True)
    multiply(3, 0, 0)
    multiply(3, 1, 0)
    arrived(ring["B", 4] + ring["A", "table", 4])
    hand(4, 0)
    drain(12)
    arrived(handed[3, 1])
    late(3, 0, 1)
    unpack(3, 1, 1, 1)

    def hand_last(lo, n):
        return send(mine4.at[pl.ds(lo, n)], theirs4.at[pl.ds(lo, n)], cdev)

    crossed[4].wait_recv()
    last = [hand_last(*back)]
    arrived(ring["C", "table", 4])
    last.append(send(table_of(1, 4, 0), table_of(1, 4, 0), cdev))
    for copy, part in zip(ring["C", 4], halves_of("C")):
        copy.wait_recv()
        last.append(hand_last(*part))
    arrived(handed[4, 0])
    unpack(4, 0, 0, 0, unroll=True)
    multiply(3, 1, 1)
    unpack_last(mine4, core, 0, unroll=True)
    multiply(4, 0, 0)
    multiply_last(core, 0)
    drain(4)
    arrived(last)
    unpack_last(theirs4, 1 - core, 1, unroll=True)
    multiply_last(1 - core, 1)

    lane = lax.broadcasted_iota(jnp.int32, (1, WIDTH), 1)
    fetch[1].wait()

    def square(i, total):
        rows = pl.ds(pl.multiple_of(i * T, T), T)
        keep = jnp.where(lane < T, kt[0, i], kt[1, i]).astype(jnp.float32)
        v = acc[rows, :]
        v = v * v * keep
        acc[rows, :] = v
        return total + jnp.sum(v.reshape(T // 8, 8, WIDTH), axis=0)

    part = lax.fori_loop(0, RT, square, jnp.zeros((8, WIDTH), jnp.float32), unroll=True)
    cs[me_row] = jnp.sum(part, axis=0, keepdims=True)
    sums = [send(cs.at[me_row], cs.at[me_row], dev) for dev in peers]
    drain(len(sums))
    arrived(sums)
    total = jnp.sum(cs[...], axis=0)
    scale = jnp.float32(NZ * BLOCK) / total

    def finish(i, _):
        rows = pl.ds(pl.multiple_of(i * T, T), T)
        out[rows, :] = (acc[rows, :] * scale).astype(jnp.bfloat16)
        return 0

    lax.fori_loop(0, RT, finish, 0, unroll=True)
    drain()


def body(markov, input_tiles, keep_tiles):
    hbm = pl.BlockSpec(memory_space=pltpu.HBM)

    def packed(*lead):
        return pltpu.VMEM((*lead, PACKED + 2, HALF, T), jnp.bfloat16)

    sides = [packed(1, 2), packed(2, 2), packed(2, 2), packed(2, 2), packed(1, 2)]

    return pl.pallas_call(
        kernel,
        out_shape=jax.ShapeDtypeStruct(markov.shape, jnp.bfloat16),
        in_specs=[hbm, hbm, hbm],
        out_specs=pl.BlockSpec(memory_space=pltpu.VMEM),
        scratch_shapes=sides + sides[:4]
        + [packed(), packed()]
        + [packed(1), packed(1), packed(2), packed(2), packed(1), packed(1)]
        + [
            pltpu.VMEM((NZ * BLOCK, WIDTH), jnp.bfloat16),
            pltpu.VMEM((EARLY + 2, BLOCK, 2 * WIDTH), jnp.bfloat16),
            pltpu.VMEM((BLOCK, WIDTH), jnp.float32),
            pltpu.VMEM((NROW, 1, WIDTH), jnp.float32),
            pltpu.VMEM((CT * RT, T, T), jnp.bfloat16),
            pltpu.SMEM((CT, RT), jnp.int32),
            pltpu.SMEM((CT, RT), jnp.int32),
            pltpu.SMEM((32, 128), jnp.int32),
            pltpu.SMEM((NROW, 128), jnp.int32),
            pltpu.SemaphoreType.DMA((4,)),
            pltpu.SemaphoreType.DMA((COPIES,)),
            pltpu.SemaphoreType.DMA((COPIES,)),
        ],
        compiler_params=pltpu.CompilerParams(
            collective_id=0, has_side_effects=True, vmem_limit_bytes=53 * 2**20
        ),
        name="cluster_step",
    )(markov.reshape(RT, T, WIDTH), input_tiles.T, keep_tiles.T)


def solution(mesh):
    specs = (P("row", "col"), P("row", "col"), P("row", "col"))
    return jax.shard_map(body, mesh=mesh, in_specs=specs, out_specs=P("row", "col"), check_vma=False)
```

```python
import jax
import jax.numpy as jnp
from jax import lax
from jax.experimental import pallas as pl
from jax.experimental.pallas import tpu as pltpu
from jax.sharding import PartitionSpec as P

MESH = pl.DeviceIdType.MESH
T = 128
RT, CT = 8, 2
SLOTS = 8
HALF = T // 2
PACKED = 2 * SLOTS
FRONT = 9
NZ, NY, NROW = 8, 4, 8
BLOCK = RT * T
WIDTH = CT * T
COPIES = 112
EARLY = 6


def kernel(
    mk_hbm, it_hbm, kt_hbm, out, own0, own1, own2, own3, own4, far0, far1, far2, far3, mine4, theirs4, c0, cx, cy, cyx, c2, c2x,
    rhs, lhs, acc, cs, mk, it, kt, tabs, ctabs, insem, ssem, rsem,
):
    blocks = ((own0, own1, own2, own3, own4), (far0, far1, far2, far3, None))
    me_row, me_col = lax.axis_index("row"), lax.axis_index("col")
    xlo, y = me_row // NY, me_row % NY
    z, xh, core = me_col // 4, (me_col // 2) % 2, me_col % 2
    zdevs = [(me_row, ((z + d) % NZ) * 4 + xh * 2 + core) for d in range(1, NZ)]
    up, down = zdevs[0], zdevs[-1]
    at_y = [[(x * NY + (y + d) % NY, me_col) for d in range(NY)] for x in (xlo, 1 - xlo)]
    yup, ydown = at_y[0][1], at_y[0][3]
    xdev = (me_row, z * 4 + (1 - xh) * 2 + core)
    xldev = at_y[1][0]
    cdev = (me_row, z * 4 + xh * 2 + (1 - core))
    peers = [at_y[x][d] for x, d in ((1, 2), (1, 1), (1, 3), (0, 2), (1, 0), (0, 1), (0, 3))]

    barrier = pltpu.get_barrier_semaphore()
    near = [up, down, xdev, cdev, yup, ydown, xldev]
    for dev in near:
        pl.semaphore_signal(barrier, inc=1, device_id=dev, device_id_type=MESH)
    inputs = [(it_hbm, it), (kt_hbm, kt)]
    inputs += [(mk_hbm.at[:, :, pl.ds(k * T, T)], mk.at[pl.ds(k * RT, RT)]) for k in range(CT)]
    fetch = [pltpu.make_async_copy(src, dst, insem.at[n]) for n, (src, dst) in enumerate(inputs)]
    for n in (0, 2, 3, 1):
        fetch[n].start()

    count = [0]
    started = []

    def send(src, dst, dev):
        k = count[0]
        count[0] += 1
        copy = pltpu.make_async_remote_copy(
            src_ref=src, dst_ref=dst, send_sem=ssem.at[k], recv_sem=rsem.at[k], device_id=dev, device_id_type=MESH
        )
        copy.start()
        started.append(copy)
        return copy

    def drain(keep=0):
        while len(started) > keep:
            started.pop(0).wait_send()

    def arrived(copies):
        for copy in copies:
            copy.wait_recv()

    fetch[0].wait()
    seen = jnp.int32(0)
    place = [jnp.int32(0)] * SLOTS
    for p in range(RT * CT):
        i, k = p // CT, p % CT
        there = it[k, i] > 0
        slot = jnp.where(there, seen, SLOTS)
        tabs[core * 16, p] = 2 * slot
        ctabs[me_row, p] = 2 * slot
        for s in range(min(p + 1, SLOTS)):
            place[s] = jnp.where(slot == s, k * RT + i, place[s])
        seen = seen + there.astype(jnp.int32)
    fetch[2].wait()
    fetch[3].wait()
    for s in range(SLOTS):
        tile = mk[place[s]].reshape(2, HALF, T)
        own0[0, core, 2 * s : 2 * s + 2] = tile
        c0[0, 2 * s : 2 * s + 2] = tile
    pl.semaphore_wait(barrier, len(near))

    front, back, whole = (0, FRONT), (FRONT, PACKED - FRONT), (0, PACKED)
    streams = {"A": (0, back), "B": (0, front), "C": (1, front)}
    ring, crossed, handed = {}, {}, {}

    def at(d, side, o, part):
        if o and d == 4:
            return mine4.at[pl.ds(*part)]
        return blocks[o][d].at[side % blocks[o][d].shape[0], core, pl.ds(*part)]

    def halves_of(name):
        o, (lo, n) = streams[name]
        return (lo, n // 2), (lo + n // 2, n - n // 2)

    def rel(d, side):
        return max(2 * d - 1, 0) + (side if 0 < d < 4 else 0)

    def table_of(o, d, side, n=1, c=core):
        return tabs.at[pl.ds(c * 16 + o * 8 + rel(d, side), n)]

    def both(name, d, a, b):
        o = streams[name][0]
        return [send(at(d - 1, 0, o, a), at(d, 0, o, a), up), send(at(d - 1, 1, o, b), at(d, 1, o, b), down)]

    def hop(name, d):
        if d > 1:
            arrived(ring[name, d - 1])
        if name != "B":
            o = streams[name][0]
            arrived(ring.get((name, "table", d - 1), []))
            ways = [(0, up), (1, down)][: 2 if d < 4 else 1]
            ring[name, "table", d] = [send(table_of(o, d - 1, side), table_of(o, d, side), dev) for side, dev in ways]
        whole = streams[name][1]
        ring[name, d] = both(name, d, *(halves_of(name) if d > 2 else (whole, whole)))

    def rest(name):
        ring[name, "rest"] = both(name, 3, *reversed(halves_of(name)))

    def cross(d):
        if d == 4:
            src, dst = at(4, 0, 0, back), at(4, 0, 1, back)
        else:
            src, dst = [blocks[o][d].at[:, core, pl.ds(*back)] for o in (0, 1)]
        crossed[d] = send(src, dst, xdev)

    def hand(d, o):
        table = table_of(o, d, 0, 2 if 0 < d < 4 else 1)
        src = blocks[o][d].at[:, core, pl.ds(*whole)]
        handed[d, o] = [send(table, table, cdev), send(src, src, cdev)]

    def column(ref, n, b):
        def step(i, _):
            for k in range(CT):
                rows = pl.ds(pl.multiple_of(b * BLOCK + i * T, T), T)
                rhs[rows, k * T : (k + 1) * T] = ref[n, pl.ds(ctabs[b, i * CT + k], 2)].reshape(T, T)
            return 0

        lax.fori_loop(0, RT, step, 0)

    place_of = {}

    def unpack(d, side, o, turn=None, unroll=False):
        place_of[d, side, o] = n = len(place_of) if turn is None else EARLY + turn

        def step(i, _):
            for c in (0, 1):
                for k in range(CT):
                    slot = tabs[c * 16 + o * 8 + rel(d, side), i * CT + k]
                    tile = blocks[o][d][side, c, pl.ds(slot, 2)].reshape(T, T)
                    lhs[n, pl.ds(pl.multiple_of(i * T, T), T), c * WIDTH + k * T : c * WIDTH + (k + 1) * T] = tile
            return 0

        lax.fori_loop(0, RT, step, 0, unroll=unroll)

    def multiply(d, side, o, first=False):
        owner = (z + (NZ - d if side == 0 else d)) % NZ
        half = (1 - xh) if o else xh
        rows = pl.ds(pl.multiple_of(owner * BLOCK + half * (2 * WIDTH), 2 * WIDTH), 2 * WIDTH)
        part = jnp.dot(lhs[place_of[d, side, o]], rhs[rows, :], preferred_element_type=jnp.float32)
        acc[...] = part if first else acc[...] + part

    def late(d, side, o):
        unpack(d, side, o, side)
        multiply(d, side, o)

    def unpack_last(ref, c, n, unroll=False):
        def step(i, _):
            for k in range(CT):
                tile = ref[pl.ds(tabs[c * 16 + 8 + rel(4, 0), i * CT + k], 2)].reshape(T, T)
                lhs[n, pl.ds(pl.multiple_of(i * T, T), T), k * T : (k + 1) * T] = tile
            return 0

        lax.fori_loop(0, RT, step, 0, unroll=unroll)

    def multiply_last(c, n):
        base = ((z + 4) % NZ) * BLOCK + (1 - xh) * (2 * WIDTH) + c * WIDTH
        rows = pl.ds(pl.multiple_of(base, WIDTH), WIDTH)
        return acc[...] + jnp.dot(lhs[n, :, :WIDTH], rhs[rows, :], preferred_element_type=jnp.float32)

    def ctable(b, devs):
        return [send(ctabs.at[pl.ds(b, 1)], ctabs.at[pl.ds(b, 1)], dev) for dev in devs]

    hop("A", 1)
    tx = send(table_of(0, 0, 0), table_of(1, 0, 0), xdev)
    px = send(at(0, 0, 0, front), at(0, 0, 1, front), xdev)
    lower, upper = pl.ds(0, SLOTS), pl.ds(SLOTS, SLOTS)
    ct = ctable(me_row, [yup, ydown])
    y1 = [send(c0.at[0, part], cy.at[n, part], dev) for n, dev, part in [(0, yup, lower), (1, ydown, upper)]]
    hop("B", 1)
    y1 += [send(c0.at[0, part], cy.at[n, part], dev) for n, dev, part in [(0, yup, upper), (1, ydown, lower)]]
    ctx = ctable(me_row, [xldev])
    xl = [send(c0.at[0, part], cx.at[0, part], xldev) for part in (lower, upper)]
    hand(0, 0)
    cross(0)

    zero = jnp.zeros((2, HALF, T), jnp.bfloat16)
    for ref in blocks[0] + blocks[1][:4]:
        for n in range(ref.shape[0]):
            for c in (0, 1):
                ref[n, c, PACKED : PACKED + 2] = zero
    for ref in (mine4, theirs4):
        ref[PACKED : PACKED + 2] = zero
    for ref in (c0, cx, cy, cyx, c2, c2x):
        for n in range(ref.shape[0]):
            ref[n, PACKED : PACKED + 2] = zero

    below, above, across = (y + NY - 1) % NY, (y + 1) % NY, (y + 2) % NY
    other = (1 - xlo) * NY
    hop("A", 2)
    cross(1)
    arrived([tx, px])
    hop("C", 1)
    arrived(y1[:2] + ct)
    ct2 = ctable(xlo * NY + below, [yup])
    y2 = [send(cy.at[0, lower], c2.at[0, lower], yup), send(cy.at[1, upper], c2.at[0, upper], ydown)]
    hop("B", 2)
    hand(1, 0)
    arrived(ctx + xl[:1])
    ctyx = ctable(other + y, [yup, ydown])
    y1x = [send(cx.at[0, lower], cyx.at[n, lower], dev) for n, dev in enumerate((yup, ydown))]
    column(c0, 0, me_row)
    hop("A", 3)
    rest("A")
    cross(2)
    arrived(xl[1:])
    y1x += [send(cx.at[0, upper], cyx.at[n, upper], dev) for n, dev in enumerate((yup, ydown))]
    column(cx, 0, other + y)
    arrived(y1[2:])
    column(cy, 0, xlo * NY + below)
    column(cy, 1, xlo * NY + above)
    arrived(handed[0, 0])
    unpack(0, 0, 0)
    hop("C", 2)
    crossed[0].wait_recv()
    hand(0, 1)
    arrived(handed[1, 0])
    unpack(1, 0, 0)
    unpack(1, 1, 0)
    arrived([y1x[0], y1x[3]] + ctyx)
    ct2x = ctable(other + below, [yup])
    y2x = [send(cyx.at[0, lower], c2x.at[0, lower], yup), send(cyx.at[1, upper], c2x.at[0, upper], ydown)]
    hop("B", 3)
    hand(2, 0)
    arrived(y1x[1:3])
    column(cyx, 0, other + below)
    column(cyx, 1, other + above)
    hop("A", 4)
    arrived(ring["A", "rest"])
    cross(3)
    arrived(handed[0, 1])
    unpack(0, 0, 1)
    arrived(y2 + ct2)
    column(c2, 0, xlo * NY + across)
    crossed[1].wait_recv()
    hand(1, 1)
    arrived(handed[2, 0])
    unpack(2, 0, 0)
    unpack(2, 1, 0)
    drain(24)
    arrived(y2x + ct2x)
    column(c2x, 0, other + across)
    multiply(0, 0, 0, first=True)
    multiply(1, 0, 0)
    hop("C", 3)
    rest("B")
    rest("C")
    multiply(1, 1, 0)
    multiply(0, 0, 1)
    hop("B", 4)
    multiply(2, 0, 0)
    drain(20)
    crossed[2].wait_recv()
    hand(2, 1)
    multiply(2, 1, 0)
    arrived(handed[1, 1])
    late(1, 0, 1)
    arrived(ring["A", 4])
    cross(4)
    late(1, 1, 1)
    hop("C", 4)
    arrived(handed[2, 1])
    late(2, 0, 1)
    arrived(ring["B", "rest"])
    hand(3, 0)
    late(2, 1, 1)
    drain(16)
    arrived(ring["C", "rest"])
    crossed[3].wait_recv()
    hand(3, 1)
    arrived(handed[3, 0])
    unpack(3, 0, 0, 0)
    unpack(3, 1, 0, 1, unroll=True)
    multiply(3, 0, 0)
    multiply(3, 1, 0)
    arrived(ring["B", 4] + ring["A", "table", 4])
    hand(4, 0)
    drain(12)
    arrived(handed[3, 1])
    late(3, 0, 1)
    unpack(3, 1, 1, 1)

    def hand_last(lo, n):
        return send(mine4.at[pl.ds(lo, n)], theirs4.at[pl.ds(lo, n)], cdev)

    crossed[4].wait_recv()
    last = [hand_last(*back)]
    arrived(ring["C", "table", 4])
    last.append(send(table_of(1, 4, 0), table_of(1, 4, 0), cdev))
    for copy, part in zip(ring["C", 4], halves_of("C")):
        copy.wait_recv()
        last.append(hand_last(*part))
    arrived(handed[4, 0])
    unpack(4, 0, 0, 0, unroll=True)
    multiply(3, 1, 1)
    unpack_last(mine4, core, 0, unroll=True)
    multiply(4, 0, 0)
    acc[...] = multiply_last(core, 0)
    drain(4)
    arrived(last)
    unpack_last(theirs4, 1 - core, 1, unroll=True)
    product = multiply_last(1 - core, 1)

    lane = lax.broadcasted_iota(jnp.int32, (1, WIDTH), 1)
    fetch[1].wait()
    part = jnp.zeros((8, WIDTH), jnp.float32)
    for i in range(RT):
        keep = jnp.where(lane < T, kt[0, i], kt[1, i]).astype(jnp.float32)
        v = product[i * T : (i + 1) * T]
        v = v * v * keep
        acc[i * T : (i + 1) * T] = v
        part = part + jnp.sum(v.reshape(T // 8, 8, WIDTH), axis=0)
    cs[me_row] = jnp.sum(part, axis=0, keepdims=True)
    sums = [send(cs.at[me_row], cs.at[me_row], dev) for dev in peers]
    drain(len(sums))
    arrived(sums)
    total = jnp.sum(cs[...], axis=0)
    scale = jnp.float32(NZ * BLOCK) / total

    def finish(i, _):
        rows = pl.ds(pl.multiple_of(i * T, T), T)
        out[rows, :] = (acc[rows, :] * scale).astype(jnp.bfloat16)
        return 0

    lax.fori_loop(0, RT, finish, 0, unroll=True)
    drain()


def body(markov, input_tiles, keep_tiles):
    hbm = pl.BlockSpec(memory_space=pltpu.HBM)

    def packed(*lead):
        return pltpu.VMEM((*lead, PACKED + 2, HALF, T), jnp.bfloat16)

    sides = [packed(1, 2), packed(2, 2), packed(2, 2), packed(2, 2), packed(1, 2)]

    return pl.pallas_call(
        kernel,
        out_shape=jax.ShapeDtypeStruct(markov.shape, jnp.bfloat16),
        in_specs=[hbm, hbm, hbm],
        out_specs=pl.BlockSpec(memory_space=pltpu.VMEM),
        scratch_shapes=sides + sides[:4]
        + [packed(), packed()]
        + [packed(1), packed(1), packed(2), packed(2), packed(1), packed(1)]
        + [
            pltpu.VMEM((NZ * BLOCK, WIDTH), jnp.bfloat16),
            pltpu.VMEM((EARLY + 2, BLOCK, 2 * WIDTH), jnp.bfloat16),
            pltpu.VMEM((BLOCK, WIDTH), jnp.float32),
            pltpu.VMEM((NROW, 1, WIDTH), jnp.float32),
            pltpu.VMEM((CT * RT, T, T), jnp.bfloat16),
            pltpu.SMEM((CT, RT), jnp.int32),
            pltpu.SMEM((CT, RT), jnp.int32),
            pltpu.SMEM((32, 128), jnp.int32),
            pltpu.SMEM((NROW, 128), jnp.int32),
            pltpu.SemaphoreType.DMA((4,)),
            pltpu.SemaphoreType.DMA((COPIES,)),
            pltpu.SemaphoreType.DMA((COPIES,)),
        ],
        compiler_params=pltpu.CompilerParams(
            collective_id=0, has_side_effects=True, vmem_limit_bytes=53 * 2**20
        ),
        name="cluster_step",
    )(markov.reshape(RT, T, WIDTH), input_tiles.T, keep_tiles.T)


def solution(mesh):
    specs = (P("row", "col"), P("row", "col"), P("row", "col"))
    return jax.shard_map(body, mesh=mesh, in_specs=specs, out_specs=P("row", "col"), check_vma=False)
```
